32 devices in a mesh: tm: 16 (over z, y, x), space: 2 (over core).
Axes of the slice: x: 2, y: 2, z: 4, core: 2. Of those that a mesh axis runs over, the one named last changes fastest.
Arguments:
- image_gradient: bfloat16 [32, 128, 3, 4096], P('tm', 'space'), may hold values from -0.375 to 0.375
- residual: bfloat16 [32, 128, 4096], P('tm', 'space'), may hold values from -6 to 6
- phase: float32 [32], P('tm'), may hold values from 0 to 1
- counts: int32 [128], P('space'), may hold values from 512 to 4096
- owner: int32 [128, 1], P('space'), may hold values from 0 to 1, as said below
Outputs:
- hessian_blocks: float32 [32, 192, 576], P('tm', 'space')
- gradient_blocks: float32 [32, 192, 24], P('tm', 'space')
The draws below stay inside these ranges and needn't reach their ends.
Inputs may be any that keep to these rules, and one draw needn't show every extreme that they name: Among the 64 bricks of each aligned block at most 48 share an owner, and one owner takes exactly 48 bricks of every block.
All inputs are finite; a program needn't handle non-finite values.
Results may differ from the reference program's by a relative error of at most 0.0029.
Values sent between devices are 32-bit elements; how exact they have to be, the bound alone decides.
No kernel may reach another device: no remote copies, remote signals or barrier semaphores. Data moves between devices by JAX's collectives and lax.ppermute only.
A program may use at most 64 MiB of HBM per device.

```python
import jax
import jax.numpy as jnp
from jax import lax

EDGE = 16
VOX = 4096
SPD = 24
BR = 64
STEPS = 32
BRICKS = 128
CAP = 48
SLOTS = 192
N_SPACE = 2


def draw_image_gradient(key, part):
    shape = (STEPS, BRICKS, 3, VOX)
    common_shape = (STEPS, BRICKS, 1, VOX)
    lone_entry = jnp.clip(jax.random.normal(jax.random.fold_in(key, 31), shape, jnp.float32), -4.0, 4.0)
    common_across = jnp.clip(jax.random.normal(jax.random.fold_in(key, 32), common_shape, jnp.float32), -4.0, 4.0)
    return ((lone_entry + common_across) * 3.0 * VOX ** (-0.5)).astype(jnp.bfloat16)


def draw_owner(key, part):
    owners = BRICKS // BR
    label_count = owners * CAP
    labels = jnp.arange(label_count, dtype=jnp.int32) // CAP
    busiest = jax.random.randint(jax.random.fold_in(key, 7), (), 0, owners)

    def one_block(block):
        block_key = jax.random.fold_in(jax.random.fold_in(key, 13), block)
        order_first = jax.random.permutation(block_key, label_count)
        picked = labels[order_first]
        spots = jnp.arange(label_count, dtype=jnp.int32)
        priority = jnp.where(picked == busiest, spots, label_count + spots)
        chosen = picked[jnp.argsort(priority, stable=True)][:BR]
        return chosen[jax.random.permutation(jax.random.fold_in(block_key, 1), BR)]
    return jax.vmap(one_block)(jnp.arange(owners, dtype=jnp.int32)).reshape(BRICKS, 1).astype(jnp.int32)


def with_ends(array, stream_key, least, largest):
    spot = [jax.random.randint(jax.random.fold_in(stream_key, axis), (), 0, length) for axis, length in enumerate(array.shape)]
    main_axis = array.shape.index(max(array.shape))
    beside = spot[:main_axis] + [(spot[main_axis] + 1) % array.shape[main_axis]] + spot[main_axis + 1:]
    return array.at[tuple(spot)].set(least).at[tuple(beside)].set(largest)


def shard_levels(rng, shape, split, low, largest):
    def one(axis_at, blocks):
        heights = jax.random.uniform(jax.random.fold_in(jax.random.fold_in(rng, 6), axis_at), (blocks,), jnp.float32, low / len(split), largest / len(split))
        return jnp.repeat(jnp.exp(heights), shape[axis_at] // blocks).reshape((-1,) + (1,) * (len(shape) - axis_at - 1))

    factor_of = one(*split[0])
    for cut in split[1:]:
        factor_of = factor_of * one(*cut)
    return factor_of


def centred(stream_key, dims, scale, reach, cuts=(), held_as=jnp.bfloat16):
    factor_of = shard_levels(stream_key, dims, cuts, -0.22, 0.18) if cuts else 1.0
    entries = jax.random.normal(stream_key, dims, jnp.float32) * scale * factor_of
    return jnp.minimum(jnp.maximum(entries, -reach), reach).astype(held_as)


def setup_inputs(seed: int = 0) -> dict:
    key_list = jax.random.split(jax.random.key(seed), 6)
    return {
        "image_gradient": draw_image_gradient(jax.random.fold_in(key_list[5], 71), 0),
        "residual": centred(key_list[1], (STEPS, BRICKS, VOX), 1.0, 6.0, ((0, 16), (1, 2))),
        "phase": jnp.clip(1.0 * jax.random.uniform(key_list[2], (STEPS,), jnp.float32) ** shard_levels(key_list[2], (STEPS,), ((0, 16),), -0.2, 0.2), 0.0, 1.0),
        "counts": with_ends(jax.random.randint(key_list[3], (BRICKS,), VOX // 8, VOX + 1), jax.random.fold_in(key_list[3], 1), VOX // 8, VOX).astype(jnp.int32),
        "owner": draw_owner(jax.random.fold_in(key_list[5], 71), 0),
    }


def spline_weights(phase):
    u = phase.astype(jnp.float32)
    return jnp.stack([(1.0 - u) ** 3 / 6.0, (3.0 * u ** 3 - 6.0 * u ** 2 + 4.0) / 6.0,
                      (-3.0 * u ** 3 + 3.0 * u ** 2 + 3.0 * u + 1.0) / 6.0, u ** 3 / 6.0], axis=-1)


def shape_table(edge):
    voxel = jnp.arange(edge * edge * edge, dtype=jnp.int32)
    first = ((voxel // (edge * edge)).astype(jnp.float32) + 0.5) / edge
    second = (((voxel // edge) % edge).astype(jnp.float32) + 0.5) / edge
    third = ((voxel % edge).astype(jnp.float32) + 0.5) / edge
    rows = []
    for node in range(8):
        along_first = first if (node >> 2) & 1 else 1.0 - first
        along_second = second if (node >> 1) & 1 else 1.0 - second
        along_third = third if node & 1 else 1.0 - third
        rows.append(along_first * along_second * along_third)
    return jnp.stack(rows, axis=0)


def reference(image_gradient, residual, phase, counts, owner):
    valid_mask = lax.broadcasted_iota(jnp.int32, (BRICKS, VOX), 1) < counts[:, None]
    shapes = shape_table(EDGE)

    def per_step(pair):
        grads, resid = pair
        product = shapes[None, :, None, :] * grads.astype(jnp.float32)[:, None, :, :]
        sens = product.reshape(BRICKS, SPD, VOX).astype(jnp.bfloat16)
        masked = jnp.where(valid_mask[:, None, :], sens, jnp.zeros((), jnp.bfloat16))
        wide = masked.astype(jnp.float32)
        hessian = jnp.einsum("bdv,bev->bde", wide, wide, precision=lax.Precision.HIGHEST).reshape(BRICKS, SPD * SPD)
        gradient = jnp.einsum("bdv,bv->bd", wide, resid.astype(jnp.float32), precision=lax.Precision.HIGHEST)
        return hessian, gradient

    step_hessian, step_gradient = lax.map(per_step, (image_gradient, residual))
    weights = spline_weights(phase)
    target = jnp.clip(jnp.arange(STEPS, dtype=jnp.int32)[:, None] - 1 + jnp.arange(4, dtype=jnp.int32)[None, :], 0, STEPS - 1)
    hits_table = (target[:, :, None] == jnp.arange(STEPS, dtype=jnp.int32)[None, None, :]).astype(jnp.float32)
    basis_lookup_grid = jnp.einsum("tj,tjk->tk", weights, hits_table, precision=lax.Precision.HIGHEST)
    coef_hessian = jnp.einsum("tk,tbf->kbf", basis_lookup_grid * basis_lookup_grid, step_hessian, precision=lax.Precision.HIGHEST)
    coef_gradient = jnp.einsum("tk,tbf->kbf", basis_lookup_grid, step_gradient, precision=lax.Precision.HIGHEST)
    owner_flat = owner[:, 0].astype(jnp.int32)
    block_owner = owner_flat.reshape(N_SPACE, BR)
    owner_hits = (block_owner[:, :, None] == jnp.arange(N_SPACE, dtype=jnp.int32)[None, None, :]).astype(jnp.int32)
    earlier = jnp.cumsum(owner_hits, axis=1) - owner_hits
    brick_rank = jnp.sum(earlier * owner_hits, axis=2).reshape(BRICKS).astype(jnp.int32)
    source = (jnp.arange(BRICKS, dtype=jnp.int32) // BR).astype(jnp.int32)
    slot_index = owner_flat * (N_SPACE * CAP) + source * CAP + brick_rank
    hessian_blocks = jnp.zeros((STEPS, SLOTS, SPD * SPD), jnp.float32).at[:, slot_index].set(coef_hessian)
    gradient_blocks = jnp.zeros((STEPS, SLOTS, SPD), jnp.float32).at[:, slot_index].set(coef_gradient)
    return hessian_blocks, gradient_blocks
```

```python
import functools
import math

import ml_dtypes
import numpy as np
import jax
import jax.numpy as jnp
from jax import lax
from jax.experimental import pallas as pl
from jax.experimental.pallas import tpu as pltpu
from jax.sharding import PartitionSpec as P

LANES = 128
QUADS = 27
NODES = 8
SLOT = 32
WIDTH = 2 * LANES
GRAD_AT = 6 * SLOT
DEST_AT = WIDTH - 1
LOW_AT = 64
BF16 = jnp.bfloat16
F32 = jnp.float32


def component_pairs(comps):
    return [(c, e) for c in range(comps) for e in range(c, comps)]


@functools.cache
def voxel_tables(voxels):
    edge = round(voxels ** (1 / 3))
    at = (np.arange(edge) + 0.5) / edge
    lines = np.stack([1 - at, at])
    quads = np.stack([(1 - at) ** 2, at * (1 - at), at * at])
    shapes = np.einsum("ai,bj,ck->abcijk", lines, lines, lines).reshape(NODES, voxels)
    squares = np.einsum("ai,bj,ck->abcijk", quads, quads, quads).reshape(QUADS, voxels)
    scale = (1 + np.floor(128 * np.modf(np.arange(voxels) * 0.6180339887498949)[0]) / 128).reshape(1, voxels)
    rows = np.concatenate([squares / scale, shapes])
    high = rows.astype(ml_dtypes.bfloat16)
    low = (rows - high.astype(np.float64)).astype(ml_dtypes.bfloat16)
    table = np.zeros((voxels, LANES), ml_dtypes.bfloat16)
    table[:, : QUADS + NODES] = high.T
    table[:, LOW_AT : LOW_AT + QUADS + NODES] = low.T
    return table, scale.astype(ml_dtypes.bfloat16)


@functools.cache
def expansion_tables(comps):
    dofs = NODES * comps
    pairs = component_pairs(comps)
    hessian = np.zeros((WIDTH, dofs * dofs), ml_dtypes.bfloat16)
    gradient = np.zeros((dofs, WIDTH), ml_dtypes.bfloat16)
    for d in range(dofs):
        a, c = divmod(d, comps)
        gradient[d, GRAD_AT + NODES * c + a] = 1
        for f in range(dofs):
            b, e = divmod(f, comps)
            quad = sum(((a >> k & 1) + (b >> k & 1)) * 3**k for k in range(3))
            hessian[SLOT * pairs.index((min(c, e), max(c, e))) + quad, d * dofs + f] = 1
    return hessian, gradient


def spline_weights(phase):
    return [
        (1.0 - phase) ** 3 / 6.0,
        (3.0 * phase**3 - 6.0 * phase**2 + 4.0) / 6.0,
        (-3.0 * phase**3 + 3.0 * phase**2 + 3.0 * phase + 1.0) / 6.0,
        phase**3 / 6.0,
    ]


def column(row):
    n = row.shape[1]
    eye = lax.broadcasted_iota(jnp.int32, (n, n), 0) == lax.broadcasted_iota(jnp.int32, (n, n), 1)
    return jnp.sum(jnp.where(eye, jnp.broadcast_to(row, (n, n)), 0.0), axis=1, keepdims=True)


def moments_kernel(
    chunk,
    capacity,
    grads_hbm,
    resid_hbm,
    counts_hbm,
    owner_hbm,
    phase_hbm,
    table_hbm,
    scale_hbm,
    own_ref,
    send_a_ref,
    send_b_ref,
    grads,
    resid,
    counts_ref,
    owner_ref,
    phase_ref,
    table,
    scale,
    products_a,
    products_b,
    moments,
    small_sems,
    sems,
):
    steps, comps, bricks, voxels = grads.shape
    pairs = component_pairs(comps)
    groups = len(pairs) + 2 * comps
    small = [
        pltpu.make_async_copy(src, dst, small_sems.at[i])
        for i, (src, dst) in enumerate(
            [
                (counts_hbm, counts_ref),
                (owner_hbm, owner_ref),
                (phase_hbm, phase_ref),
                (scale_hbm, scale),
                (table_hbm, table),
            ]
        )
    ]
    parts = []
    for s in range(steps):
        for b in range(0, bricks, chunk):
            i = 2 * len(parts)
            rows = pl.ds(b, chunk)
            parts.append(
                (
                    s,
                    b,
                    pltpu.make_async_copy(grads_hbm.at[s, :, rows], grads.at[s, :, rows], sems.at[i]),
                    pltpu.make_async_copy(resid_hbm.at[s, rows], resid.at[s, rows], sems.at[i + 1]),
                )
            )
    for copy in small:
        copy.start()
    for _, _, grads_copy, resid_copy in parts:
        grads_copy.start()
        resid_copy.start()

    lane = lax.broadcasted_iota(jnp.int32, (1, LANES), 1)

    def fill(s, b, products):
        rows = slice(b, b + chunk)
        limit = jnp.broadcast_to(counts[rows], (chunk, LANES)).astype(jnp.int16)
        zero = jnp.zeros((), BF16)
        for at in range(0, voxels, LANES):
            cols = slice(at, at + LANES)
            voxel = lax.broadcasted_iota(jnp.int16, (chunk, LANES), 1) + jnp.int16(at)
            valid = voxel < limit
            scale_here = jnp.where(valid, jnp.broadcast_to(scale[:, cols], (chunk, LANES)), zero)
            resid_here = jnp.where(valid, resid[s, rows, cols], zero).astype(F32)
            g = [grads[s, c, rows, cols] for c in range(comps)]
            scaled = [x * scale_here for x in g]
            blocks = [scaled[c] * g[e] for c, e in pairs]
            for c in range(comps):
                exact = g[c].astype(F32) * resid_here
                high = exact.astype(BF16)
                blocks += [high, (exact - high.astype(F32)).astype(BF16)]
            for i, block in enumerate(blocks):
                products[i * chunk : (i + 1) * chunk, cols] = block

    def reduce(s, b, products):
        sums = jnp.dot(products[...], table[...], preferred_element_type=F32)
        halves = [jnp.zeros((chunk, LANES), F32) for _ in range(2)]
        whole = [sums[i * chunk : (i + 1) * chunk] for i in range(len(pairs))]
        for c in range(comps):
            i = len(pairs) + 2 * c
            whole.append(sums[i * chunk : (i + 1) * chunk] + sums[(i + 1) * chunk : (i + 2) * chunk])
        for i, block in enumerate(whole):
            block = block + pltpu.roll(block, LANES - LOW_AT, 1)
            if i < len(pairs):
                source, goal, span = 0, SLOT * i, QUADS
            else:
                source, goal, span = QUADS, GRAD_AT + NODES * (i - len(pairs)), NODES
            half, goal = divmod(goal, LANES)
            shift = (goal - source) % LANES
            if shift:
                block = pltpu.roll(block, shift, 1)
            keep = (lane >= goal) & (lane < goal + span)
            halves[half] = jnp.where(keep, block, halves[half])
        for half in range(2):
            moments[s, b : b + chunk, half * LANES : (half + 1) * LANES] = halves[half]

    for copy in small[:4]:
        copy.wait()
    counts = column(counts_ref[...].astype(F32)).astype(jnp.int32)
    owner_row = owner_ref[...].astype(F32)
    owner_col = column(owner_row)
    square = (bricks, bricks)
    earlier = lax.broadcasted_iota(jnp.int32, square, 1) < lax.broadcasted_iota(jnp.int32, square, 0)
    same = (owner_col == owner_row) & earlier
    rank = jnp.sum(jnp.where(same, 1.0, 0.0), axis=1, keepdims=True)
    destination = owner_col * capacity + rank

    buffers = (products_a, products_b)
    for i, (s, b, grads_copy, resid_copy) in enumerate(parts):
        grads_copy.wait()
        resid_copy.wait()
        if i == 1:
            small[4].wait()
        fill(s, b, buffers[i % 2])
        if i:
            before = parts[i - 1]
            reduce(before[0], before[1], buffers[(i - 1) % 2])
    if len(parts) == 1:
        small[4].wait()
    reduce(parts[-1][0], parts[-1][1], buffers[(len(parts) - 1) % 2])

    place = lax.axis_index("tm")
    places = lax.axis_size("tm")
    first_step = place * steps
    weights = [spline_weights(phase_ref[:, s : s + 1]) for s in range(steps)]

    def coefficient(position):
        total = [jnp.zeros((bricks, LANES), F32) for _ in range(2)]
        for s in range(steps):
            basis = jnp.zeros((1, 1), F32)
            for j in range(4):
                reach = s - 1 + j
                if position not in (reach, max(reach, 0), min(reach, steps - 1)):
                    continue
                goal = jnp.clip(first_step + reach, 0, places * steps - 1) - first_step
                basis = basis + jnp.where(goal == position, weights[s][j], 0.0)
            squared = basis * basis
            factors = [
                jnp.broadcast_to(squared, (1, LANES)),
                jnp.where(lane < GRAD_AT - LANES, squared, basis),
            ]
            for half in range(2):
                total[half] += factors[half] * moments[s, :, half * LANES : (half + 1) * LANES]
        return total

    odd = place % 2 == 1
    empty = [jnp.zeros((bricks, LANES), F32) for _ in range(2)]
    above = [coefficient(steps + k) if k < 2 else empty for k in range(steps)]
    below = [coefficient(-1) if k == steps - 1 else empty for k in range(steps)]
    for k in range(steps):
        mine = coefficient(k)
        mine[1] = jnp.where(lane == DEST_AT - LANES, destination, mine[1])
        for half in range(2):
            cols = slice(half * LANES, (half + 1) * LANES)
            own_ref[k, :, cols] = mine[half]
            send_a_ref[k, :, cols] = jnp.where(odd, below[k][half], above[k][half])
            send_b_ref[k, :, cols] = jnp.where(odd, above[k][half], below[k][half])


def split3(x):
    high = x.astype(BF16)
    rest = x - high.astype(F32)
    middle = rest.astype(BF16)
    return high, middle, (rest - middle.astype(F32)).astype(BF16)


def expand_kernel(capacity, count, *refs):
    blocks = refs[:count]
    hessian_table, gradient_table, hessian_ref, gradient_ref = refs[count:]
    steps, bricks, _ = blocks[0].shape
    slots = hessian_ref.shape[1]
    me = lax.axis_index("space")
    slot = lax.broadcasted_iota(jnp.int32, (bricks, slots), 1).astype(F32)
    picks = []
    for distance, block in enumerate(blocks):
        source = (me + count - distance) % count
        rank = block[0, :, DEST_AT : DEST_AT + 1] - (me * capacity).astype(F32)
        mine = (rank >= 0.0) & (rank < capacity)
        goal = jnp.where(mine, rank + (source * capacity).astype(F32), -1.0)
        picks.append(jnp.where(slot == goal, 1.0, 0.0))
    pick = jnp.concatenate(picks, axis=0).astype(BF16)
    for k in range(steps):
        values = jnp.concatenate([block[k] for block in blocks], axis=0)
        hessian = gradient = None
        for part in split3(values):
            placed = lax.dot_general(
                pick, part, (((0,), (0,)), ((), ())), preferred_element_type=F32
            ).astype(BF16)
            wide = jnp.dot(placed, hessian_table[...], preferred_element_type=F32)
            thin = lax.dot_general(
                gradient_table[...], placed, (((1,), (1,)), ((), ())), preferred_element_type=F32
            )
            hessian = wide if hessian is None else hessian + wide
            gradient = thin if gradient is None else gradient + thin
        hessian_ref[k] = hessian
        gradient_ref[k] = gradient


def per_device(image_gradient, residual, phase, counts, owner):
    steps, bricks, comps, voxels = image_gradient.shape
    spaces = lax.axis_size("space")
    places = lax.axis_size("tm")
    capacity = 3 * bricks // (2 * spaces)
    dofs = NODES * comps
    chunk = math.gcd(bricks, 32)
    groups = len(component_pairs(comps)) + 2 * comps
    table, scale = voxel_tables(voxels)
    block = (steps, bricks, WIDTH)
    chunks = steps * bricks // chunk
    any_space = pl.BlockSpec(memory_space=pl.ANY)
    own, send_a, send_b = pl.pallas_call(
        functools.partial(moments_kernel, chunk, capacity),
        in_specs=[any_space] * 7,
        out_shape=[pltpu.VMEM(block, F32)] * 3,
        scratch_shapes=[
            pltpu.VMEM((steps, comps, bricks, voxels), BF16),
            pltpu.VMEM((steps, bricks, voxels), BF16),
            pltpu.VMEM((1, bricks), jnp.int32),
            pltpu.VMEM((1, bricks), jnp.int32),
            pltpu.VMEM((1, steps), F32),
            pltpu.VMEM((voxels, LANES), BF16),
            pltpu.VMEM((1, voxels), BF16),
            pltpu.VMEM((groups * chunk, voxels), BF16),
            pltpu.VMEM((groups * chunk, voxels), BF16),
            pltpu.VMEM(block, F32),
            pltpu.SemaphoreType.DMA((5,)),
            pltpu.SemaphoreType.DMA((2 * chunks,)),
        ],
        compiler_params=pltpu.CompilerParams(vmem_limit_bytes=32 << 20),
        name="moments",
    )(
        jnp.transpose(image_gradient, (0, 2, 1, 3)),
        residual,
        counts.reshape(1, bricks),
        owner.reshape(1, bricks),
        phase.reshape(1, steps),
        jnp.asarray(table),
        jnp.asarray(scale),
    )

    def exchange(values, start):
        lower = range(start, places - 1, 2)
        route = [(i, i + 1) for i in lower] + [(i + 1, i) for i in lower]
        return lax.ppermute(values, "tm", route) if route else jnp.zeros_like(values)

    total = own + exchange(send_a, 0) + exchange(send_b, 1)
    blocks = [total]
    for distance in range(1, spaces):
        route = [(i, (i + distance) % spaces) for i in range(spaces)]
        blocks.append(lax.ppermute(total, "space", route))
    hessian_table, gradient_table = expansion_tables(comps)
    hessian, gradient = pl.pallas_call(
        functools.partial(expand_kernel, capacity, spaces),
        out_shape=[
            jax.ShapeDtypeStruct((steps, spaces * capacity, dofs * dofs), F32),
            jax.ShapeDtypeStruct((steps, dofs, spaces * capacity), F32),
        ],
        compiler_params=pltpu.CompilerParams(vmem_limit_bytes=16 << 20),
        name="expand",
    )(*blocks, jnp.asarray(hessian_table), jnp.asarray(gradient_table))
    return hessian, jnp.transpose(gradient, (0, 2, 1))


def solution(mesh):
    in_specs = (
        P("tm", "space", None, None),
        P("tm", "space", None),
        P("tm"),
        P("space"),
        P("space", None),
    )
    out_specs = (P("tm", "space", None), P("tm", "space", None))
    return jax.shard_map(
        per_device, mesh=mesh, in_specs=in_specs, out_specs=out_specs, check_vma=False
    )
```

```python
import functools
import math

import ml_dtypes
import numpy as np
import jax
import jax.numpy as jnp
from jax import lax
from jax.experimental import pallas as pl
from jax.experimental.pallas import tpu as pltpu
from jax.sharding import PartitionSpec as P

LANES = 128
QUADS = 27
NODES = 8
PER_HALF = 3
GRAD_AT = PER_HALF * QUADS
WIDTH = 2 * LANES
DEST_AT = WIDTH - 1
BF16 = jnp.bfloat16
F32 = jnp.float32


def component_pairs(comps):
    return [(c, e) for c in range(comps) for e in range(c, comps)]


@functools.cache
def voxel_tables(voxels):
    edge = round(voxels ** (1 / 3))
    at = (np.arange(edge) + 0.5) / edge
    lines = np.stack([1 - at, at])
    quads = np.stack([(1 - at) ** 2, at * (1 - at), at * at])
    shapes = np.einsum("ai,bj,ck->abcijk", lines, lines, lines).reshape(NODES, voxels)
    squares = np.einsum("ai,bj,ck->abcijk", quads, quads, quads).reshape(QUADS, voxels)
    scale = (1 + np.floor(128 * np.modf(np.arange(voxels) * 0.6180339887498949)[0]) / 128).reshape(1, voxels)
    squares = (squares / scale).astype(ml_dtypes.bfloat16)
    high = shapes.astype(ml_dtypes.bfloat16)
    low = (shapes - high.astype(np.float64)).astype(ml_dtypes.bfloat16)
    table = np.zeros((LANES, voxels), ml_dtypes.bfloat16)
    rows = np.concatenate([squares] * PER_HALF + [high, low] * 2)
    table[: len(rows)] = rows
    return np.ascontiguousarray(table.T), np.repeat(scale.astype(ml_dtypes.bfloat16), 16, axis=0)


def pair_place(i):
    return i // PER_HALF, i % PER_HALF * QUADS, QUADS


def gradient_place(c):
    return c % 2, GRAD_AT + c // 2 * 2 * NODES, 2 * NODES


@functools.cache
def expansion_tables(comps):
    dofs = NODES * comps
    pairs = component_pairs(comps)
    hessian = np.zeros((WIDTH, dofs * dofs), ml_dtypes.bfloat16)
    gradient = np.zeros((dofs, WIDTH), ml_dtypes.bfloat16)
    for d in range(dofs):
        a, c = divmod(d, comps)
        half, at, _ = gradient_place(c)
        gradient[d, [half * LANES + at + a, half * LANES + at + NODES + a]] = 1
        for f in range(dofs):
            b, e = divmod(f, comps)
            quad = sum(((a >> k & 1) + (b >> k & 1)) * 3**k for k in range(3))
            half, at, _ = pair_place(pairs.index((min(c, e), max(c, e))))
            hessian[half * LANES + at + quad, d * dofs + f] = 1
    return hessian, gradient


def spline_weights(phase):
    return [
        (1.0 - phase) ** 3 / 6.0,
        (3.0 * phase**3 - 6.0 * phase**2 + 4.0) / 6.0,
        (-3.0 * phase**3 + 3.0 * phase**2 + 3.0 * phase + 1.0) / 6.0,
        phase**3 / 6.0,
    ]


def column(row):
    n = row.shape[1]
    eye = lax.broadcasted_iota(jnp.int32, (n, n), 0) == lax.broadcasted_iota(jnp.int32, (n, n), 1)
    return jnp.sum(jnp.where(eye, jnp.broadcast_to(row, (n, n)), 0.0), axis=1, keepdims=True)


def moments_kernel(
    capacity,
    grads_hbm,
    resid_hbm,
    counts_hbm,
    owner_hbm,
    phase_hbm,
    table_hbm,
    scale_hbm,
    own_ref,
    send_a_ref,
    send_b_ref,
    grads,
    resid,
    counts_ref,
    owner_ref,
    phase_ref,
    table,
    scale,
    products_a,
    products_b,
    limits,
    sums,
    moments,
    small_sems,
    sems,
):
    steps, comps, bricks, voxels = grads.shape
    pairs = component_pairs(comps)
    groups = len(pairs) + comps
    rows = steps * bricks
    plane = round(voxels ** (2 / 3))
    width = products_a.shape[1]
    buffers = (products_a, products_b)
    parts = voxels // width
    small = [
        pltpu.make_async_copy(src, dst, small_sems.at[i])
        for i, (src, dst) in enumerate(
            [
                (counts_hbm, counts_ref),
                (owner_hbm, owner_ref),
                (phase_hbm, phase_ref),
                (scale_hbm, scale),
            ]
        )
    ]

    def copies(k):
        cols = pl.ds(pl.multiple_of(k * width, width), width)
        return (
            pltpu.make_async_copy(grads_hbm.at[:, :, :, cols], grads.at[:, :, :, cols], sems.at[k, 0]),
            pltpu.make_async_copy(resid_hbm.at[:, :, cols], resid.at[:, :, cols], sems.at[k, 1]),
            pltpu.make_async_copy(table_hbm.at[cols], table.at[cols], sems.at[k, 2]),
        )

    for copy in small:
        copy.start()
    for k in range(parts):
        for copy in copies(k):
            copy.start()

    lane = lax.broadcasted_iota(jnp.int32, (1, LANES), 1)
    tall = math.gcd(bricks, 16)
    voxel = lax.broadcasted_iota(jnp.int16, (tall, plane), 1)
    zero = jnp.zeros((), BF16)

    def fill(k, products):
        start = k * width
        for b in range(0, bricks, tall):
            limit = (limits[b : b + tall] - start).astype(jnp.int16)
            left = [[None] * comps for _ in range(steps)]
            for p in range(0, width, plane):
                cols = pl.ds(pl.multiple_of(start + p, plane), plane)
                valid = voxel + jnp.int16(p) < limit
                scale_here = jnp.where(valid, scale[:tall, cols], zero)
                for s in range(steps):
                    resid_here = jnp.where(valid, resid[s, b : b + tall, cols], zero).astype(F32)
                    g = [grads[s, c, b : b + tall, cols] for c in range(comps)]
                    scaled = [x * scale_here for x in g]
                    blocks = [scaled[c] * g[e] for c, e in pairs]
                    for c in range(comps):
                        exact = g[c].astype(F32) * resid_here
                        if left[s][c] is not None:
                            exact = exact + left[s][c]
                        blocks.append(exact.astype(BF16))
                        left[s][c] = exact - blocks[-1].astype(F32)
                    for i, block in enumerate(blocks):
                        at = i * rows + s * bricks + b
                        products[at : at + tall, p : p + plane] = block

    def reduce(k, products):
        cols = pl.ds(pl.multiple_of(k * width, width), width)
        sums[...] += jnp.dot(products[...], table[cols], preferred_element_type=F32)

    for copy in small:
        copy.wait()
    counts = column(counts_ref[...].astype(F32)).astype(jnp.int32)
    limits[...] = jnp.broadcast_to(counts, (bricks, plane))
    owner_row = owner_ref[...].astype(F32)
    owner_col = column(owner_row)
    square = (bricks, bricks)
    earlier = lax.broadcasted_iota(jnp.int32, square, 1) < lax.broadcasted_iota(jnp.int32, square, 0)
    same = (owner_col == owner_row) & earlier
    rank = jnp.sum(jnp.where(same, 1.0, 0.0), axis=1, keepdims=True)
    destination = owner_col * capacity + rank
    sums[...] = jnp.zeros_like(sums)

    for k in range(parts):
        for copy in copies(k):
            copy.wait()
    for k in range(parts):
        fill(k, buffers[k % 2])
        reduce(k, buffers[k % 2])

    for s in range(steps):
        halves = [jnp.zeros((bricks, LANES), F32) for _ in range(2)]
        for i in range(groups):
            half, goal, span = pair_place(i) if i < len(pairs) else gradient_place(i - len(pairs))
            keep = (lane >= goal) & (lane < goal + span)
            at = i * rows + s * bricks
            halves[half] = jnp.where(keep, sums[at : at + bricks], halves[half])
        for half in range(2):
            moments[s, :, half * LANES : (half + 1) * LANES] = halves[half]

    place = lax.axis_index("tm")
    places = lax.axis_size("tm")
    first_step = place * steps
    weights = [spline_weights(phase_ref[:, s : s + 1]) for s in range(steps)]

    def coefficient(position):
        total = [jnp.zeros((bricks, LANES), F32) for _ in range(2)]
        for s in range(steps):
            basis = jnp.zeros((1, 1), F32)
            for j in range(4):
                reach = s - 1 + j
                if position not in (reach, max(reach, 0), min(reach, steps - 1)):
                    continue
                goal = jnp.clip(first_step + reach, 0, places * steps - 1) - first_step
                basis = basis + jnp.where(goal == position, weights[s][j], 0.0)
            squared = basis * basis
            factor = jnp.where(lane < GRAD_AT, squared, basis)
            for half in range(2):
                total[half] += factor * moments[s, :, half * LANES : (half + 1) * LANES]
        return total

    odd = place % 2 == 1
    empty = [jnp.zeros((bricks, LANES), F32) for _ in range(2)]
    above = [coefficient(steps + k) if k < 2 else empty for k in range(steps)]
    below = [coefficient(-1) if k == steps - 1 else empty for k in range(steps)]
    for k in range(steps):
        mine = coefficient(k)
        mine[1] = jnp.where(lane == DEST_AT - LANES, destination, mine[1])
        for half in range(2):
            cols = slice(half * LANES, (half + 1) * LANES)
            own_ref[k, :, cols] = mine[half]
            send_a_ref[k, :, cols] = jnp.where(odd, below[k][half], above[k][half])
            send_b_ref[k, :, cols] = jnp.where(odd, above[k][half], below[k][half])


def split3(x):
    high = x.astype(BF16)
    rest = x - high.astype(F32)
    middle = rest.astype(BF16)
    return high, middle, (rest - middle.astype(F32)).astype(BF16)


def expand_kernel(capacity, count, *refs):
    blocks = refs[:count]
    hessian_table, gradient_table, hessian_ref, gradient_ref = refs[count:]
    steps, bricks, _ = blocks[0].shape
    slots = hessian_ref.shape[1]
    me = lax.axis_index("space")
    slot = lax.broadcasted_iota(jnp.int32, (bricks, slots), 1).astype(F32)
    picks = []
    for distance, block in enumerate(blocks):
        source = (me + count - distance) % count
        rank = block[0, :, DEST_AT : DEST_AT + 1] - (me * capacity).astype(F32)
        mine = (rank >= 0.0) & (rank < capacity)
        goal = jnp.where(mine, rank + (source * capacity).astype(F32), -1.0)
        picks.append(jnp.where(slot == goal, 1.0, 0.0))
    pick = jnp.concatenate(picks, axis=0).astype(BF16)
    for k in range(steps):
        values = jnp.concatenate([block[k] for block in blocks], axis=0)
        hessian = gradient = None
        for part in split3(values):
            placed = lax.dot_general(
                pick, part, (((0,), (0,)), ((), ())), preferred_element_type=F32
            ).astype(BF16)
            wide = jnp.dot(placed, hessian_table[...], preferred_element_type=F32)
            thin = lax.dot_general(
                gradient_table[...], placed, (((1,), (1,)), ((), ())), preferred_element_type=F32
            )
            hessian = wide if hessian is None else hessian + wide
            gradient = thin if gradient is None else gradient + thin
        hessian_ref[k] = hessian
        gradient_ref[k] = gradient


def per_device(image_gradient, residual, phase, counts, owner):
    steps, bricks, comps, voxels = image_gradient.shape
    spaces = lax.axis_size("space")
    places = lax.axis_size("tm")
    capacity = 3 * bricks // (2 * spaces)
    dofs = NODES * comps
    groups = len(component_pairs(comps)) + comps
    parts = 2
    width = voxels // parts
    table, scale = voxel_tables(voxels)
    block = (steps, bricks, WIDTH)
    in_hbm = pl.BlockSpec(memory_space=pltpu.HBM)
    own, send_a, send_b = pl.pallas_call(
        functools.partial(moments_kernel, capacity),
        in_specs=[in_hbm] * 7,
        out_shape=[pltpu.VMEM(block, F32)] * 3,
        scratch_shapes=[
            pltpu.VMEM((steps, comps, bricks, voxels), BF16),
            pltpu.VMEM((steps, bricks, voxels), BF16),
            pltpu.VMEM((1, bricks), jnp.int32),
            pltpu.VMEM((1, bricks), jnp.int32),
            pltpu.VMEM((1, steps), F32),
            pltpu.VMEM((voxels, LANES), BF16),
            pltpu.VMEM(scale.shape, BF16),
            pltpu.VMEM((groups * steps * bricks, width), BF16),
            pltpu.VMEM((groups * steps * bricks, width), BF16),
            pltpu.VMEM((bricks, round(voxels ** (2 / 3))), jnp.int32),
            pltpu.VMEM((groups * steps * bricks, LANES), F32),
            pltpu.VMEM(block, F32),
            pltpu.SemaphoreType.DMA((4,)),
            pltpu.SemaphoreType.DMA((parts, 3)),
        ],
        compiler_params=pltpu.CompilerParams(vmem_limit_bytes=32 << 20),
        name="moments",
    )(
        *(
            pltpu.with_memory_space_constraint(x, pltpu.HBM)
            for x in (
                jnp.transpose(image_gradient, (0, 2, 1, 3)),
                residual,
                counts.reshape(1, bricks),
                owner.reshape(1, bricks),
                phase.reshape(1, steps),
                jnp.asarray(table),
                jnp.asarray(scale),
            )
        )
    )

    def exchange(values, start):
        lower = range(start, places - 1, 2)
        route = [(i, i + 1) for i in lower] + [(i + 1, i) for i in lower]
        return lax.ppermute(values, "tm", route) if route else jnp.zeros_like(values)

    total = own + exchange(send_a, 0) + exchange(send_b, 1)
    blocks = [total]
    for distance in range(1, spaces):
        route = [(i, (i + distance) % spaces) for i in range(spaces)]
        blocks.append(lax.ppermute(total, "space", route))
    hessian_table, gradient_table = expansion_tables(comps)
    hessian, gradient = pl.pallas_call(
        functools.partial(expand_kernel, capacity, spaces),
        out_shape=[
            jax.ShapeDtypeStruct((steps, spaces * capacity, dofs * dofs), F32),
            jax.ShapeDtypeStruct((steps, dofs, spaces * capacity), F32),
        ],
        compiler_params=pltpu.CompilerParams(vmem_limit_bytes=16 << 20),
        name="expand",
    )(*blocks, jnp.asarray(hessian_table), jnp.asarray(gradient_table))
    return hessian, jnp.transpose(gradient, (0, 2, 1))


def solution(mesh):
    in_specs = (
        P("tm", "space", None, None),
        P("tm", "space", None),
        P("tm"),
        P("space"),
        P("space", None),
    )
    out_specs = (P("tm", "space", None), P("tm", "space", None))
    return jax.shard_map(
        per_device, mesh=mesh, in_specs=in_specs, out_specs=out_specs, check_vma=False
    )
```

```python
import functools
import math

import ml_dtypes
import numpy as np
import jax
import jax.numpy as jnp
from jax import lax
from jax.experimental import pallas as pl
from jax.experimental.pallas import tpu as pltpu
from jax.sharding import PartitionSpec as P

LANES = 128
QUADS = 27
NODES = 8
PER_HALF = 3
GRAD_AT = PER_HALF * QUADS
BF16 = jnp.bfloat16
F32 = jnp.float32


def component_pairs(comps):
    return [(c, e) for c in range(comps) for e in range(c, comps)]


@functools.cache
def voxel_tables(voxels):
    edge = round(voxels ** (1 / 3))
    at = (np.arange(edge) + 0.5) / edge
    lines = np.stack([1 - at, at])
    quads = np.stack([(1 - at) ** 2, at * (1 - at), at * at])
    shapes = np.einsum("ai,bj,ck->abcijk", lines, lines, lines).reshape(NODES, voxels)
    squares = np.einsum("ai,bj,ck->abcijk", quads, quads, quads).reshape(QUADS, voxels)
    scale = (1 + np.floor(128 * np.modf(np.arange(voxels) * 0.6180339887498949)[0]) / 128).reshape(1, voxels)
    squares = (squares / scale).astype(ml_dtypes.bfloat16)
    high = shapes.astype(ml_dtypes.bfloat16)
    low = (shapes - high.astype(np.float64)).astype(ml_dtypes.bfloat16)
    table = np.zeros((LANES, voxels), ml_dtypes.bfloat16)
    rows = np.concatenate([squares] * PER_HALF + [high, high, low, low])
    table[: len(rows)] = rows
    return np.ascontiguousarray(table.T), np.repeat(scale.astype(ml_dtypes.bfloat16), 16, axis=0)


def voxel_parts(voxels, sixteenths):
    ends = np.cumsum((0,) + sixteenths) * (voxels // 16)
    return tuple((int(a), int(b - a)) for a, b in zip(ends, ends[1:]))


def pair_place(i):
    return i // PER_HALF, i % PER_HALF * QUADS, QUADS


def gradient_place(c):
    return c % 2, GRAD_AT + c // 2 * NODES, NODES


@functools.cache
def packing(steps, comps):
    ends = [0, 0]
    places = [pair_place(i) for i in range(len(component_pairs(comps)))]
    for half, at, count in places + [gradient_place(c) for c in range(comps)]:
        ends[half] = max(ends[half], at + count)
    groups = -(-(steps * sum(ends) + 1) // LANES)
    free = [[g, 0, LANES - (g == groups - 1)] for g in range(groups)]
    pieces = []
    for step, half in sorted(np.ndindex(steps, 2), key=lambda x: -ends[x[1]]):
        source, left = 0, ends[half]
        while left:
            gap = max(free, key=lambda f: (f[1] + left <= f[2], f[1] == 0, f[2] - f[1]))
            count = min(left, gap[2] - gap[1])
            pieces.append((step, half, source, gap[0], gap[1], count))
            gap[1] += count
            source += count
            left -= count
    return groups, tuple(pieces)


def packed_lane(pieces, step, half, lane):
    for s, h, source, group, goal, count in pieces:
        if (s, h) == (step, half) and source <= lane < source + count:
            return group * LANES + goal + lane - source


@functools.cache
def expansion_tables(steps, comps):
    dofs = NODES * comps
    pairs = component_pairs(comps)
    groups, pieces = packing(steps, comps)
    hessian = np.zeros((steps, groups * LANES, dofs * dofs), ml_dtypes.bfloat16)
    gradient = np.zeros((steps * dofs, groups * LANES), ml_dtypes.bfloat16)
    for k in range(steps):
        for d in range(dofs):
            a, c = divmod(d, comps)
            half, at, _ = gradient_place(c)
            gradient[k * dofs + d, packed_lane(pieces, k, half, at + a)] = 1
            for f in range(dofs):
                b, e = divmod(f, comps)
                quad = sum(((a >> n & 1) + (b >> n & 1)) * 3**n for n in range(3))
                half, at, _ = pair_place(pairs.index((min(c, e), max(c, e))))
                hessian[k, packed_lane(pieces, k, half, at + quad), d * dofs + f] = 1
    return hessian, gradient


def spline_weights(phase):
    return [
        (1.0 - phase) ** 3 / 6.0,
        (3.0 * phase**3 - 6.0 * phase**2 + 4.0) / 6.0,
        (-3.0 * phase**3 + 3.0 * phase**2 + 3.0 * phase + 1.0) / 6.0,
        phase**3 / 6.0,
    ]


def column(row):
    n = row.shape[1]
    eye = lax.broadcasted_iota(jnp.int32, (n, n), 0) == lax.broadcasted_iota(jnp.int32, (n, n), 1)
    return jnp.sum(jnp.where(eye, jnp.broadcast_to(row, (n, n)), 0.0), axis=1, keepdims=True)


def moments_kernel(
    capacity,
    parts,
    ahead,
    grads_hbm,
    resid_hbm,
    counts_hbm,
    owner_hbm,
    phase_hbm,
    table_hbm,
    scale_hbm,
    own_ref,
    send_a_ref,
    send_b_ref,
    grads,
    resid,
    counts_ref,
    owner_ref,
    phase_ref,
    table,
    scale,
    products_a,
    products_b,
    limits,
    sums,
    moments,
    small_sems,
    sems,
):
    steps, comps, bricks, voxels = grads.shape
    pairs = component_pairs(comps)
    groups = len(pairs) + comps
    rows = steps * bricks
    plane = round(voxels ** (2 / 3))
    buffers = (products_a, products_b)
    small = [
        pltpu.make_async_copy(src, dst, small_sems.at[i])
        for i, (src, dst) in enumerate(
            [
                (counts_hbm, counts_ref),
                (owner_hbm, owner_ref),
                (phase_hbm, phase_ref),
                (scale_hbm, scale),
            ]
        )
    ]

    def copies(k):
        start, width = parts[k]
        cols = pl.ds(start, width)
        return (
            pltpu.make_async_copy(grads_hbm.at[:, :, :, cols], grads.at[:, :, :, cols], sems.at[k, 0]),
            pltpu.make_async_copy(resid_hbm.at[:, :, cols], resid.at[:, :, cols], sems.at[k, 1]),
            pltpu.make_async_copy(table_hbm.at[cols], table.at[cols], sems.at[k, 2]),
        )

    for copy in small:
        copy.start()
    for k in range(ahead):
        for copy in copies(k):
            copy.start()

    lane = lax.broadcasted_iota(jnp.int32, (1, LANES), 1)
    tall = math.gcd(bricks, 16)
    voxel = lax.broadcasted_iota(jnp.int16, (tall, plane), 1)
    zero = jnp.zeros((), BF16)

    def fill(k, products):
        start, width = parts[k]
        for b in range(0, bricks, tall):
            limit = (limits[b : b + tall] - start).astype(jnp.int16)
            left = [[None] * comps for _ in range(steps)]
            for p in range(0, width, plane):
                cols = slice(start + p, start + p + plane)
                valid = voxel + jnp.int16(p) < limit
                scale_here = jnp.where(valid, scale[:tall, cols], zero)
                for s in range(steps):
                    resid_here = jnp.where(valid, resid[s, b : b + tall, cols], zero).astype(F32)
                    g = [grads[s, c, b : b + tall, cols] for c in range(comps)]
                    scaled = [x * scale_here for x in g]
                    blocks = [scaled[c] * g[e] for c, e in pairs]
                    for c in range(comps):
                        exact = g[c].astype(F32) * resid_here
                        if left[s][c] is not None:
                            exact = exact + left[s][c]
                        blocks.append(exact.astype(BF16))
                        left[s][c] = exact - blocks[-1].astype(F32)
                    for i, block in enumerate(blocks):
                        at = i * rows + s * bricks + b
                        products[at : at + tall, p : p + plane] = block

    def reduce(k, products):
        start, width = parts[k]
        for at in range(0, groups * rows, groups * rows // 2):
            here = slice(at, at + groups * rows // 2)
            part = jnp.dot(products[here, :width], table[start : start + width], preferred_element_type=F32)
            sums[here] = part if k == 0 else sums[here] + part

    for copy in small:
        copy.wait()
    counts = column(counts_ref[...].astype(F32)).astype(jnp.int32)
    limits[...] = jnp.broadcast_to(counts, (bricks, plane))
    owner_row = owner_ref[...].astype(F32)
    owner_col = column(owner_row)
    square = (bricks, bricks)
    earlier = lax.broadcasted_iota(jnp.int32, square, 1) < lax.broadcasted_iota(jnp.int32, square, 0)
    same = (owner_col == owner_row) & earlier
    rank = jnp.sum(jnp.where(same, 1.0, 0.0), axis=1, keepdims=True)
    destination = owner_col * capacity + rank

    for k in range(len(parts)):
        for copy in copies(k):
            copy.wait()
        if k + ahead < len(parts):
            for copy in copies(k + ahead):
                copy.start()
        fill(k, buffers[k % 2])
        reduce(k, buffers[k % 2])

    doubled = (comps + 1) // 2 * NODES
    for s in range(steps):
        halves = [jnp.zeros((bricks, LANES), F32) for _ in range(2)]
        for i in range(groups):
            at = i * rows + s * bricks
            block = sums[at : at + bricks]
            if i < len(pairs):
                half, goal, span = pair_place(i)
                keep = (lane >= goal) & (lane < goal + span)
            else:
                half, goal, span = gradient_place(i - len(pairs))
                keep = (lane >= goal) & (lane < goal + span)
                keep |= (lane >= goal + doubled) & (lane < goal + doubled + span)
            halves[half] = jnp.where(keep, block, halves[half])
        for half in range(2):
            low = pltpu.roll(halves[half], LANES - doubled, 1)
            whole = halves[half] + jnp.where(lane >= GRAD_AT, low, 0.0)
            moments[s, :, half * LANES : (half + 1) * LANES] = whole

    place = lax.axis_index("tm")
    places = lax.axis_size("tm")
    first_step = place * steps
    weights = [spline_weights(phase_ref[:, s : s + 1]) for s in range(steps)]

    def coefficient(position):
        total = [jnp.zeros((bricks, LANES), F32) for _ in range(2)]
        for s in range(steps):
            basis = jnp.zeros((1, 1), F32)
            for j in range(4):
                reach = s - 1 + j
                if position not in (reach, max(reach, 0), min(reach, steps - 1)):
                    continue
                goal = jnp.clip(first_step + reach, 0, places * steps - 1) - first_step
                basis = basis + jnp.where(goal == position, weights[s][j], 0.0)
            squared = basis * basis
            factor = jnp.where(lane < GRAD_AT, squared, basis)
            for half in range(2):
                total[half] += factor * moments[s, :, half * LANES : (half + 1) * LANES]
        return total

    packed_groups, pieces = packing(steps, comps)

    def pack(slabs):
        packed = [jnp.zeros((bricks, LANES), F32) for _ in range(packed_groups)]
        for k, half, source, group, goal, count in pieces:
            if slabs[k] is None:
                continue
            block = slabs[k][half]
            if goal != source:
                block = pltpu.roll(block, (goal - source) % LANES, 1)
            keep = (lane >= goal) & (lane < goal + count)
            packed[group] = jnp.where(keep, block, packed[group])
        return packed

    odd = place % 2 == 1
    above = pack([coefficient(steps + k) if k < 2 else None for k in range(steps)])
    below = pack([coefficient(-1) if k == steps - 1 else None for k in range(steps)])
    mine = pack([coefficient(k) for k in range(steps)])
    mine[-1] = jnp.where(lane == LANES - 1, destination, mine[-1])
    for group in range(packed_groups):
        cols = slice(group * LANES, (group + 1) * LANES)
        send_b_ref[:, cols] = jnp.where(odd, above[group], below[group])
        send_a_ref[:, cols] = jnp.where(odd, below[group], above[group])
        own_ref[:, cols] = mine[group]


def split(x):
    high = x.astype(BF16)
    rest = x - high.astype(F32)
    middle = rest.astype(BF16)
    return high, middle, (rest - middle.astype(F32)).astype(BF16)


def expand_kernel(capacity, count, *refs):
    blocks = refs[:count]
    hessian_table, gradient_table, hessian_ref, gradient_ref = refs[count:]
    bricks, width = blocks[0].shape
    steps, slots, _ = hessian_ref.shape
    dofs = gradient_ref.shape[1]
    me = lax.axis_index("space")
    slot = lax.broadcasted_iota(jnp.int32, (bricks, slots), 1).astype(F32)
    picks = []
    for distance, block in enumerate(blocks):
        source = (me + count - distance) % count
        rank = block[:, width - 1 :] - (me * capacity).astype(F32)
        mine = (rank >= 0.0) & (rank < capacity)
        goal = jnp.where(mine, rank + (source * capacity).astype(F32), -1.0)
        picks.append(jnp.where(slot == goal, 1.0, 0.0))
    pick = jnp.concatenate(picks, axis=0).astype(BF16)
    values = jnp.concatenate([block[...] for block in blocks], axis=0)
    placed = [
        lax.dot_general(pick, part, (((0,), (0,)), ((), ())), preferred_element_type=F32).astype(BF16)
        for part in split(values)
    ]
    for k in range(steps):
        hessian_ref[k] = sum(
            jnp.dot(part, hessian_table[k], preferred_element_type=F32) for part in placed
        )
    gradient = sum(
        lax.dot_general(gradient_table[...], part, (((1,), (1,)), ((), ())), preferred_element_type=F32)
        for part in placed
    )
    for k in range(steps):
        gradient_ref[k] = gradient[k * dofs : (k + 1) * dofs]


def per_device(image_gradient, residual, phase, counts, owner):
    steps, bricks, comps, voxels = image_gradient.shape
    spaces = lax.axis_size("space")
    places = lax.axis_size("tm")
    capacity = 3 * bricks // (2 * spaces)
    dofs = NODES * comps
    groups = len(component_pairs(comps)) + comps
    parts = voxel_parts(voxels, (4, 4, 4, 4))
    widest = max(width for _, width in parts)
    table, scale = voxel_tables(voxels)
    block = (bricks, packing(steps, comps)[0] * LANES)
    in_hbm = pl.BlockSpec(memory_space=pltpu.HBM)
    own, send_a, send_b = pl.pallas_call(
        functools.partial(moments_kernel, capacity, parts, 2),
        in_specs=[in_hbm] * 7,
        out_shape=[pltpu.VMEM(block, F32)] * 3,
        scratch_shapes=[
            pltpu.VMEM((steps, comps, bricks, voxels), BF16),
            pltpu.VMEM((steps, bricks, voxels), BF16),
            pltpu.VMEM((1, bricks), jnp.int32),
            pltpu.VMEM((1, bricks), jnp.int32),
            pltpu.VMEM((1, steps), F32),
            pltpu.VMEM((voxels, LANES), BF16),
            pltpu.VMEM(scale.shape, BF16),
            pltpu.VMEM((groups * steps * bricks, widest), BF16),
            pltpu.VMEM((groups * steps * bricks, widest), BF16),
            pltpu.VMEM((bricks, round(voxels ** (2 / 3))), jnp.int32),
            pltpu.VMEM((groups * steps * bricks, LANES), F32),
            pltpu.VMEM((steps, bricks, 2 * LANES), F32),
            pltpu.SemaphoreType.DMA((4,)),
            pltpu.SemaphoreType.DMA((len(parts), 3)),
        ],
        compiler_params=pltpu.CompilerParams(vmem_limit_bytes=32 << 20),
        name="moments",
    )(
        *(
            pltpu.with_memory_space_constraint(x, pltpu.HBM)
            for x in (
                jnp.transpose(image_gradient, (0, 2, 1, 3)),
                residual,
                counts.reshape(1, bricks),
                owner.reshape(1, bricks),
                phase.reshape(1, steps),
                jnp.asarray(table),
                jnp.asarray(scale),
            )
        )
    )

    def exchange(values, start):
        lower = range(start, places - 1, 2)
        route = [(i, i + 1) for i in lower] + [(i + 1, i) for i in lower]
        return lax.ppermute(values, "tm", route) if route else jnp.zeros_like(values)

    total = own + exchange(send_a, 0) + exchange(send_b, 1)
    blocks = [total]
    for distance in range(1, spaces):
        route = [(i, (i + distance) % spaces) for i in range(spaces)]
        blocks.append(lax.ppermute(total, "space", route))
    hessian_table, gradient_table = expansion_tables(steps, comps)
    hessian, gradient = pl.pallas_call(
        functools.partial(expand_kernel, capacity, spaces),
        out_shape=[
            jax.ShapeDtypeStruct((steps, spaces * capacity, dofs * dofs), F32),
            jax.ShapeDtypeStruct((steps, dofs, spaces * capacity), F32),
        ],
        compiler_params=pltpu.CompilerParams(vmem_limit_bytes=16 << 20),
        name="expand",
    )(*blocks, jnp.asarray(hessian_table), jnp.asarray(gradient_table))
    return hessian, jnp.transpose(gradient, (0, 2, 1))


def solution(mesh):
    in_specs = (
        P("tm", "space", None, None),
        P("tm", "space", None),
        P("tm"),
        P("space"),
        P("space", None),
    )
    out_specs = (P("tm", "space", None), P("tm", "space", None))
    return jax.shard_map(
        per_device, mesh=mesh, in_specs=in_specs, out_specs=out_specs, check_vma=False
    )
```

```python
import functools
import math

import ml_dtypes
import numpy as np
import jax
import jax.numpy as jnp
from jax import lax
from jax.experimental import pallas as pl
from jax.experimental.pallas import tpu as pltpu
from jax.sharding import PartitionSpec as P

LANES = 128
QUADS = 27
NODES = 8
PER_HALF = 3
GRAD_AT = PER_HALF * QUADS
BF16 = jnp.bfloat16
F32 = jnp.float32


def component_pairs(comps):
    return [(c, e) for c in range(comps) for e in range(c, comps)]


@functools.cache
def voxel_tables(voxels):
    edge = round(voxels ** (1 / 3))
    at = (np.arange(edge) + 0.5) / edge
    lines = np.stack([1 - at, at])
    quads = np.stack([(1 - at) ** 2, at * (1 - at), at * at])
    shapes = np.einsum("ai,bj,ck->abcijk", lines, lines, lines).reshape(NODES, voxels)
    squares = np.einsum("ai,bj,ck->abcijk", quads, quads, quads).reshape(QUADS, voxels)
    scale = (1 + np.floor(128 * np.modf(np.arange(voxels) * 0.6180339887498949)[0]) / 128).reshape(1, voxels)
    squares = (squares / scale).astype(ml_dtypes.bfloat16)
    high = shapes.astype(ml_dtypes.bfloat16)
    low = (shapes - high.astype(np.float64)).astype(ml_dtypes.bfloat16)
    table = np.zeros((LANES, voxels), ml_dtypes.bfloat16)
    rows = np.concatenate([squares] * PER_HALF + [high, high, low, low])
    table[: len(rows)] = rows
    return np.ascontiguousarray(table.T), np.repeat(scale.astype(ml_dtypes.bfloat16), 16, axis=0)


def voxel_parts(voxels, sixteenths):
    ends = np.cumsum((0,) + sixteenths) * (voxels // 16)
    return tuple((int(a), int(b - a)) for a, b in zip(ends, ends[1:]))


def pair_place(i):
    return i // PER_HALF, i % PER_HALF * QUADS, QUADS


def gradient_place(c):
    return c % 2, GRAD_AT + c // 2 * NODES, NODES


@functools.cache
def packing(steps, comps):
    ends = [0, 0]
    places = [pair_place(i) for i in range(len(component_pairs(comps)))]
    for half, at, count in places + [gradient_place(c) for c in range(comps)]:
        ends[half] = max(ends[half], at + count)
    groups = -(-(steps * sum(ends) + 1) // LANES)
    free = [[g, 0, LANES - (g == groups - 1)] for g in range(groups)]
    pieces = []
    for step, half in sorted(np.ndindex(steps, 2), key=lambda x: -ends[x[1]]):
        source, left = 0, ends[half]
        while left:
            gap = max(free, key=lambda f: (f[1] + left <= f[2], f[1] == 0, f[2] - f[1]))
            count = min(left, gap[2] - gap[1])
            pieces.append((step, half, source, gap[0], gap[1], count))
            gap[1] += count
            source += count
            left -= count
    return groups, tuple(pieces)


def packed_lane(pieces, step, half, lane):
    for s, h, source, group, goal, count in pieces:
        if (s, h) == (step, half) and source <= lane < source + count:
            return group * LANES + goal + lane - source


@functools.cache
def expansion_tables(steps, comps):
    dofs = NODES * comps
    pairs = component_pairs(comps)
    groups, pieces = packing(steps, comps)
    hessian = np.zeros((steps, groups * LANES, dofs * dofs), ml_dtypes.bfloat16)
    gradient = np.zeros((steps * dofs, groups * LANES), ml_dtypes.bfloat16)
    for k in range(steps):
        for d in range(dofs):
            a, c = divmod(d, comps)
            half, at, _ = gradient_place(c)
            gradient[k * dofs + d, packed_lane(pieces, k, half, at + a)] = 1
            for f in range(dofs):
                b, e = divmod(f, comps)
                quad = sum(((a >> n & 1) + (b >> n & 1)) * 3**n for n in range(3))
                half, at, _ = pair_place(pairs.index((min(c, e), max(c, e))))
                hessian[k, packed_lane(pieces, k, half, at + quad), d * dofs + f] = 1
    return hessian, gradient


def spline_weights(phase):
    return [
        (1.0 - phase) ** 3 / 6.0,
        (3.0 * phase**3 - 6.0 * phase**2 + 4.0) / 6.0,
        (-3.0 * phase**3 + 3.0 * phase**2 + 3.0 * phase + 1.0) / 6.0,
        phase**3 / 6.0,
    ]


def column(row):
    n = row.shape[1]
    eye = lax.broadcasted_iota(jnp.int32, (n, n), 0) == lax.broadcasted_iota(jnp.int32, (n, n), 1)
    return jnp.sum(jnp.where(eye, jnp.broadcast_to(row, (n, n)), 0.0), axis=1, keepdims=True)


def moments_kernel(
    capacity,
    parts,
    ahead,
    grads_hbm,
    resid_hbm,
    counts_hbm,
    owner_hbm,
    phase_hbm,
    table_hbm,
    scale_hbm,
    own_ref,
    send_a_ref,
    *refs,
):
    spaces = lax.axis_size("space")
    send_b_refs, refs = refs[:spaces], refs[spaces:]
    (
        grads,
        resid,
        counts_ref,
        owner_ref,
        phase_ref,
        table,
        scale,
        products_a,
        products_b,
        limits,
        sums,
        moments,
        small_sems,
        sems,
    ) = refs
    steps, comps, bricks, voxels = grads.shape
    pairs = component_pairs(comps)
    groups = len(pairs) + comps
    rows = steps * bricks
    plane = round(voxels ** (2 / 3))
    buffers = (products_a, products_b)
    small = [
        pltpu.make_async_copy(src, dst, small_sems.at[i])
        for i, (src, dst) in enumerate(
            [
                (counts_hbm, counts_ref),
                (owner_hbm, owner_ref),
                (phase_hbm, phase_ref),
                (scale_hbm, scale),
            ]
        )
    ]

    def copies(k):
        start, width = parts[k]
        cols = pl.ds(start, width)
        return (
            pltpu.make_async_copy(grads_hbm.at[:, :, :, cols], grads.at[:, :, :, cols], sems.at[k, 0]),
            pltpu.make_async_copy(resid_hbm.at[:, :, cols], resid.at[:, :, cols], sems.at[k, 1]),
            pltpu.make_async_copy(table_hbm.at[cols], table.at[cols], sems.at[k, 2]),
        )

    for copy in small:
        copy.start()
    for k in range(ahead):
        for copy in copies(k):
            copy.start()

    lane = lax.broadcasted_iota(jnp.int32, (1, LANES), 1)
    tall = math.gcd(bricks, 16)
    voxel = lax.broadcasted_iota(jnp.int16, (tall, plane), 1)
    zero = jnp.zeros((), BF16)

    def fill(k, products):
        start, width = parts[k]
        for b in range(0, bricks, tall):
            limit = (limits[b : b + tall] - start).astype(jnp.int16)
            left = [[None] * comps for _ in range(steps)]
            for p in range(0, width, plane):
                cols = slice(start + p, start + p + plane)
                valid = voxel + jnp.int16(p) < limit
                scale_here = jnp.where(valid, scale[:tall, cols], zero)
                for s in range(steps):
                    resid_here = jnp.where(valid, resid[s, b : b + tall, cols], zero).astype(F32)
                    g = [grads[s, c, b : b + tall, cols] for c in range(comps)]
                    scaled = [x * scale_here for x in g]
                    blocks = [scaled[c] * g[e] for c, e in pairs]
                    for c in range(comps):
                        exact = g[c].astype(F32) * resid_here
                        if left[s][c] is not None:
                            exact = exact + left[s][c]
                        blocks.append(exact.astype(BF16))
                        left[s][c] = exact - blocks[-1].astype(F32)
                    for i, block in enumerate(blocks):
                        at = i * rows + s * bricks + b
                        products[at : at + tall, p : p + plane] = block

    def reduce(k, products):
        start, width = parts[k]
        for at in range(0, groups * rows, groups * rows // 2):
            here = slice(at, at + groups * rows // 2)
            part = jnp.dot(products[here, :width], table[start : start + width], preferred_element_type=F32)
            sums[here] = part if k == 0 else sums[here] + part

    for copy in small:
        copy.wait()
    counts = column(counts_ref[...].astype(F32)).astype(jnp.int32)
    limits[...] = jnp.broadcast_to(counts, (bricks, plane))
    owner_row = owner_ref[...].astype(F32)
    owner_col = column(owner_row)
    square = (bricks, bricks)
    earlier = lax.broadcasted_iota(jnp.int32, square, 1) < lax.broadcasted_iota(jnp.int32, square, 0)
    same = (owner_col == owner_row) & earlier
    rank = jnp.sum(jnp.where(same, 1.0, 0.0), axis=1, keepdims=True)
    destination = owner_col * capacity + rank
    later = lax.broadcasted_iota(jnp.int32, square, 1) > lax.broadcasted_iota(jnp.int32, square, 0)
    before = jnp.where((owner_col == owner_row) & later, 1.0, 0.0)
    destination_row = owner_row * capacity + jnp.sum(before, axis=0, keepdims=True)
    me = lax.axis_index("space")
    slot = lax.broadcasted_iota(jnp.int32, (capacity, bricks), 0)
    picks = []
    for distance in range(spaces):
        goal = (slot + (me + distance) % spaces * capacity).astype(F32)
        picks.append(jnp.where(goal == destination_row, 1.0, 0.0).astype(BF16))

    for k in range(len(parts)):
        for copy in copies(k):
            copy.wait()
        if k + ahead < len(parts):
            for copy in copies(k + ahead):
                copy.start()
        fill(k, buffers[k % 2])
        reduce(k, buffers[k % 2])

    doubled = (comps + 1) // 2 * NODES
    for s in range(steps):
        halves = [jnp.zeros((bricks, LANES), F32) for _ in range(2)]
        for i in range(groups):
            at = i * rows + s * bricks
            block = sums[at : at + bricks]
            if i < len(pairs):
                half, goal, span = pair_place(i)
                keep = (lane >= goal) & (lane < goal + span)
            else:
                half, goal, span = gradient_place(i - len(pairs))
                keep = (lane >= goal) & (lane < goal + span)
                keep |= (lane >= goal + doubled) & (lane < goal + doubled + span)
            halves[half] = jnp.where(keep, block, halves[half])
        for half in range(2):
            low = pltpu.roll(halves[half], LANES - doubled, 1)
            whole = halves[half] + jnp.where(lane >= GRAD_AT, low, 0.0)
            moments[s, :, half * LANES : (half + 1) * LANES] = whole

    place = lax.axis_index("tm")
    places = lax.axis_size("tm")
    first_step = place * steps
    weights = [spline_weights(phase_ref[:, s : s + 1]) for s in range(steps)]

    def coefficient(position):
        total = [jnp.zeros((bricks, LANES), F32) for _ in range(2)]
        for s in range(steps):
            basis = jnp.zeros((1, 1), F32)
            for j in range(4):
                reach = s - 1 + j
                if position not in (reach, max(reach, 0), min(reach, steps - 1)):
                    continue
                goal = jnp.clip(first_step + reach, 0, places * steps - 1) - first_step
                basis = basis + jnp.where(goal == position, weights[s][j], 0.0)
            squared = basis * basis
            factor = jnp.where(lane < GRAD_AT, squared, basis)
            for half in range(2):
                total[half] += factor * moments[s, :, half * LANES : (half + 1) * LANES]
        return total

    packed_groups, pieces = packing(steps, comps)

    def pack(slabs):
        packed = [jnp.zeros((bricks, LANES), F32) for _ in range(packed_groups)]
        for k, half, source, group, goal, count in pieces:
            if slabs[k] is None:
                continue
            block = slabs[k][half]
            if goal != source:
                block = pltpu.roll(block, (goal - source) % LANES, 1)
            keep = (lane >= goal) & (lane < goal + count)
            packed[group] = jnp.where(keep, block, packed[group])
        return packed

    odd = place % 2 == 1
    above = pack([coefficient(steps + k) if k < 2 else None for k in range(steps)])
    below = pack([coefficient(-1) if k == steps - 1 else None for k in range(steps)])
    for group in range(packed_groups):
        cols = slice(group * LANES, (group + 1) * LANES)
        parts_b = split(jnp.where(odd, above[group], below[group]))
        for pick, ref in zip(picks, send_b_refs):
            ref[:, cols] = sum(jnp.dot(pick, part, preferred_element_type=F32) for part in parts_b)
        send_a_ref[:, cols] = jnp.where(odd, below[group], above[group])
    mine = pack([coefficient(k) for k in range(steps)])
    mine[-1] = jnp.where(lane == LANES - 1, destination, mine[-1])
    for group in range(packed_groups):
        own_ref[:, group * LANES : (group + 1) * LANES] = mine[group]


def split(x):
    high = x.astype(BF16)
    return high, (x - high.astype(F32)).astype(BF16)


def place_kernel(capacity, *refs):
    *blocks, out_ref = refs
    me = lax.axis_index("space")
    width = out_ref.shape[1]
    for distance, block in enumerate(blocks):
        slot = lax.broadcasted_iota(jnp.int32, (block.shape[0], capacity), 1)
        goal = (slot + me * capacity).astype(F32)
        pick = jnp.where(goal == block[:, width - 1 :], 1.0, 0.0).astype(BF16)
        out_ref[distance * capacity : (distance + 1) * capacity] = sum(
            lax.dot_general(pick, part, (((0,), (0,)), ((), ())), preferred_element_type=F32)
            for part in split(block[...])
        )


def expand_kernel(
    capacity, ready, last, table, gradient_table, hessian_hbm, gradient_hbm, total, wide, thin, sems
):
    steps, slots, _ = wide.shape
    dofs = thin.shape[1]
    spaces = slots // capacity
    me = lax.axis_index("space")
    for distance in range(spaces):
        here = slice(distance * capacity, (distance + 1) * capacity)
        source = (me + spaces - distance) % spaces
        rows = pl.ds(pl.multiple_of(source * capacity, math.gcd(capacity, 8)), capacity)
        total[rows] = ready[here] + last[here]
    parts = split(total[...])
    copies = []
    for k in range(steps):
        wide[k] = sum(jnp.dot(part, table[k], preferred_element_type=F32) for part in parts)
        copies.append(pltpu.make_async_copy(wide.at[k], hessian_hbm.at[k], sems.at[k]))
        copies[-1].start()
    gradient = sum(
        lax.dot_general(gradient_table[...], part, (((1,), (1,)), ((), ())), preferred_element_type=F32)
        for part in parts
    )
    for k in range(steps):
        thin[k] = gradient[k * dofs : (k + 1) * dofs]
    copies.append(pltpu.make_async_copy(thin, gradient_hbm, sems.at[steps]))
    copies[-1].start()
    for copy in copies:
        copy.wait()


def per_device(image_gradient, residual, phase, counts, owner):
    steps, bricks, comps, voxels = image_gradient.shape
    spaces = lax.axis_size("space")
    places = lax.axis_size("tm")
    capacity = 3 * bricks // (2 * spaces)
    dofs = NODES * comps
    groups = len(component_pairs(comps)) + comps
    parts = voxel_parts(voxels, (4, 4, 4, 4))
    widest = max(width for _, width in parts)
    table, scale = voxel_tables(voxels)
    block = (bricks, packing(steps, comps)[0] * LANES)
    in_hbm = pl.BlockSpec(memory_space=pltpu.HBM)
    own, send_a, *send_b = pl.pallas_call(
        functools.partial(moments_kernel, capacity, parts, 2),
        in_specs=[in_hbm] * 7,
        out_shape=[pltpu.VMEM(block, F32)] * 2 + [pltpu.VMEM((capacity, block[1]), F32)] * spaces,
        scratch_shapes=[
            pltpu.VMEM((steps, comps, bricks, voxels), BF16),
            pltpu.VMEM((steps, bricks, voxels), BF16),
            pltpu.VMEM((1, bricks), jnp.int32),
            pltpu.VMEM((1, bricks), jnp.int32),
            pltpu.VMEM((1, steps), F32),
            pltpu.VMEM((voxels, LANES), BF16),
            pltpu.VMEM(scale.shape, BF16),
            pltpu.VMEM((groups * steps * bricks, widest), BF16),
            pltpu.VMEM((groups * steps * bricks, widest), BF16),
            pltpu.VMEM((bricks, round(voxels ** (2 / 3))), jnp.int32),
            pltpu.VMEM((groups * steps * bricks, LANES), F32),
            pltpu.VMEM((steps, bricks, 2 * LANES), F32),
            pltpu.SemaphoreType.DMA((4,)),
            pltpu.SemaphoreType.DMA((len(parts), 3)),
        ],
        compiler_params=pltpu.CompilerParams(vmem_limit_bytes=32 << 20),
        name="moments",
    )(
        *(
            pltpu.with_memory_space_constraint(x, pltpu.HBM)
            for x in (
                jnp.transpose(image_gradient, (0, 2, 1, 3)),
                residual,
                counts.reshape(1, bricks),
                owner.reshape(1, bricks),
                phase.reshape(1, steps),
                jnp.asarray(table),
                jnp.asarray(scale),
            )
        )
    )

    def exchange(values, start):
        lower = range(start, places - 1, 2)
        route = [(i, i + 1) for i in lower] + [(i + 1, i) for i in lower]
        return lax.ppermute(values, "tm", route) if route else jnp.zeros_like(values)

    def turned(values, distance):
        route = [(i, (i + distance) % spaces) for i in range(spaces)]
        return lax.ppermute(values, "space", route) if distance else values

    for_far = jnp.concatenate([turned(x, distance) for distance, x in enumerate(send_b)])
    near = own + exchange(send_a, 0)
    last = exchange(for_far, 1)
    blocks = [turned(near, distance) for distance in range(spaces)]
    slots = spaces * capacity
    ready = pl.pallas_call(
        functools.partial(place_kernel, capacity),
        out_shape=pltpu.VMEM((slots, block[1]), F32),
        compiler_params=pltpu.CompilerParams(vmem_limit_bytes=8 << 20),
        name="place",
    )(*blocks)
    hessian_table, gradient_table = (jnp.asarray(x) for x in expansion_tables(steps, comps))
    wide = (steps, slots, dofs * dofs)
    thin = (steps, dofs, slots)
    hessian, gradient = pl.pallas_call(
        functools.partial(expand_kernel, capacity),
        out_shape=[jax.ShapeDtypeStruct(wide, F32), jax.ShapeDtypeStruct(thin, F32)],
        out_specs=[in_hbm] * 2,
        scratch_shapes=[
            pltpu.VMEM((slots, block[1]), F32),
            pltpu.VMEM(wide, F32),
            pltpu.VMEM(thin, F32),
            pltpu.SemaphoreType.DMA((steps + 1,)),
        ],
        compiler_params=pltpu.CompilerParams(vmem_limit_bytes=16 << 20),
        name="expand",
    )(ready, last, hessian_table, gradient_table)
    return hessian, jnp.transpose(gradient, (0, 2, 1))


def solution(mesh):
    in_specs = (
        P("tm", "space", None, None),
        P("tm", "space", None),
        P("tm"),
        P("space"),
        P("space", None),
    )
    out_specs = (P("tm", "space", None), P("tm", "space", None))
    return jax.shard_map(
        per_device, mesh=mesh, in_specs=in_specs, out_specs=out_specs, check_vma=False
    )
```

```python
import functools
import math

import ml_dtypes
import numpy as np
import jax
import jax.numpy as jnp
from jax import lax
from jax.experimental import pallas as pl
from jax.experimental.pallas import tpu as pltpu
from jax.sharding import PartitionSpec as P

LANES = 128
QUADS = 27
NODES = 8
PER_HALF = 3
GRAD_AT = PER_HALF * QUADS
BF16 = jnp.bfloat16
F32 = jnp.float32


def component_pairs(comps):
    return [(c, e) for c in range(comps) for e in range(c, comps)]


@functools.cache
def voxel_tables(voxels):
    edge = round(voxels ** (1 / 3))
    at = (np.arange(edge) + 0.5) / edge
    lines = np.stack([1 - at, at])
    quads = np.stack([(1 - at) ** 2, at * (1 - at), at * at])
    shapes = np.einsum("ai,bj,ck->abcijk", lines, lines, lines).reshape(NODES, voxels)
    squares = np.einsum("ai,bj,ck->abcijk", quads, quads, quads).reshape(QUADS, voxels)
    scale = (1 + np.floor(128 * np.modf(np.arange(voxels) * 0.6180339887498949)[0]) / 128).reshape(1, voxels)
    squares = (squares / scale).astype(ml_dtypes.bfloat16)
    high = shapes.astype(ml_dtypes.bfloat16)
    low = (shapes - high.astype(np.float64)).astype(ml_dtypes.bfloat16)
    table = np.zeros((LANES, voxels), ml_dtypes.bfloat16)
    rows = np.concatenate([squares] * PER_HALF + [high, high, low, low])
    table[: len(rows)] = rows
    return np.ascontiguousarray(table.T), np.repeat(scale.astype(ml_dtypes.bfloat16), 16, axis=0)


def voxel_parts(voxels, sixteenths):
    ends = np.cumsum((0,) + sixteenths) * (voxels // 16)
    return tuple((int(a), int(b - a)) for a, b in zip(ends, ends[1:]))


def pair_place(i):
    return i // PER_HALF, i % PER_HALF * QUADS, QUADS


def gradient_place(c):
    return c % 2, GRAD_AT + c // 2 * NODES, NODES


@functools.cache
def packing(steps, comps):
    ends = [0, 0]
    places = [pair_place(i) for i in range(len(component_pairs(comps)))]
    for half, at, count in places + [gradient_place(c) for c in range(comps)]:
        ends[half] = max(ends[half], at + count)
    groups = -(-(steps * sum(ends) + 1) // LANES)
    free = [[g, 0, LANES - (g == groups - 1)] for g in range(groups)]
    pieces = []
    for step, half in sorted(np.ndindex(steps, 2), key=lambda x: -ends[x[1]]):
        source, left = 0, ends[half]
        while left:
            gap = max(free, key=lambda f: (f[1] + left <= f[2], f[1] == 0, f[2] - f[1]))
            count = min(left, gap[2] - gap[1])
            pieces.append((step, half, source, gap[0], gap[1], count))
            gap[1] += count
            source += count
            left -= count
    return groups, tuple(pieces)


def packed_lane(pieces, step, half, lane):
    for s, h, source, group, goal, count in pieces:
        if (s, h) == (step, half) and source <= lane < source + count:
            return group * LANES + goal + lane - source


@functools.cache
def expansion_tables(steps, comps):
    dofs = NODES * comps
    pairs = component_pairs(comps)
    groups, pieces = packing(steps, comps)
    hessian = np.zeros((steps, groups * LANES, dofs * dofs), ml_dtypes.bfloat16)
    gradient = np.zeros((steps * dofs, groups * LANES), ml_dtypes.bfloat16)
    for k in range(steps):
        for d in range(dofs):
            a, c = divmod(d, comps)
            half, at, _ = gradient_place(c)
            gradient[k * dofs + d, packed_lane(pieces, k, half, at + a)] = 1
            for f in range(dofs):
                b, e = divmod(f, comps)
                quad = sum(((a >> n & 1) + (b >> n & 1)) * 3**n for n in range(3))
                half, at, _ = pair_place(pairs.index((min(c, e), max(c, e))))
                hessian[k, packed_lane(pieces, k, half, at + quad), d * dofs + f] = 1
    return hessian, gradient


def spline_weights(phase):
    return [
        (1.0 - phase) ** 3 / 6.0,
        (3.0 * phase**3 - 6.0 * phase**2 + 4.0) / 6.0,
        (-3.0 * phase**3 + 3.0 * phase**2 + 3.0 * phase + 1.0) / 6.0,
        phase**3 / 6.0,
    ]


def column(row):
    n = row.shape[1]
    eye = lax.broadcasted_iota(jnp.int32, (n, n), 0) == lax.broadcasted_iota(jnp.int32, (n, n), 1)
    return jnp.sum(jnp.where(eye, jnp.broadcast_to(row, (n, n)), 0.0), axis=1, keepdims=True)


def moments_kernel(
    capacity,
    parts,
    grads_hbm,
    resid_hbm,
    counts_hbm,
    owner_hbm,
    phase_hbm,
    table_hbm,
    scale_hbm,
    own_ref,
    send_a_ref,
    *refs,
):
    spaces = lax.axis_size("space")
    send_b_refs, refs = refs[:spaces], refs[spaces:]
    (
        grads,
        resid,
        counts_ref,
        owner_ref,
        phase_ref,
        table,
        scale,
        products_a,
        products_b,
        limits,
        sums,
        moments,
        small_sems,
        sems,
    ) = refs
    steps, comps, bricks, voxels = grads.shape
    pairs = component_pairs(comps)
    groups = len(pairs) + comps
    rows = steps * bricks
    plane = round(voxels ** (2 / 3))
    buffers = (products_a, products_b)
    small = [
        pltpu.make_async_copy(src, dst, small_sems.at[i])
        for i, (src, dst) in enumerate(
            [
                (counts_hbm, counts_ref),
                (owner_hbm, owner_ref),
                (phase_hbm, phase_ref),
                (scale_hbm, scale),
            ]
        )
    ]

    def copies(k):
        start, width = parts[k]
        cols = pl.ds(start, width)
        return (
            pltpu.make_async_copy(grads_hbm.at[:, :, :, cols], grads.at[:, :, :, cols], sems.at[k, 0]),
            pltpu.make_async_copy(resid_hbm.at[:, :, cols], resid.at[:, :, cols], sems.at[k, 1]),
            pltpu.make_async_copy(table_hbm.at[cols], table.at[cols], sems.at[k, 2]),
        )

    for copy in small:
        copy.start()
    for k in range(len(parts)):
        for copy in copies(k):
            copy.start(priority=min(k, 1))

    lane = lax.broadcasted_iota(jnp.int32, (1, LANES), 1)
    tall = math.gcd(bricks, 16)
    voxel = lax.broadcasted_iota(jnp.int16, (tall, plane), 1)
    zero = jnp.zeros((), BF16)

    def fill(k, products):
        start, width = parts[k]
        for b in range(0, bricks, tall):
            limit = (limits[b : b + tall] - start).astype(jnp.int16)
            left = [[None] * comps for _ in range(steps)]
            for p in range(0, width, plane):
                cols = slice(start + p, start + p + plane)
                valid = voxel + jnp.int16(p) < limit
                scale_here = jnp.where(valid, scale[:tall, cols], zero)
                for s in range(steps):
                    resid_here = jnp.where(valid, resid[s, b : b + tall, cols], zero).astype(F32)
                    g = [grads[s, c, b : b + tall, cols] for c in range(comps)]
                    scaled = [x * scale_here for x in g]
                    blocks = [scaled[c] * g[e] for c, e in pairs]
                    for c in range(comps):
                        exact = g[c].astype(F32) * resid_here
                        if left[s][c] is not None:
                            exact = exact + left[s][c]
                        blocks.append(exact.astype(BF16))
                        left[s][c] = exact - blocks[-1].astype(F32)
                    for i, block in enumerate(blocks):
                        at = i * rows + s * bricks + b
                        products[at : at + tall, p : p + plane] = block

    def reduce(k, products):
        start, width = parts[k]
        for at in range(0, groups * rows, groups * rows // 2):
            here = slice(at, at + groups * rows // 2)
            part = jnp.dot(products[here, :width], table[start : start + width], preferred_element_type=F32)
            sums[here] = part if k == 0 else sums[here] + part

    for copy in small:
        copy.wait()
    counts = column(counts_ref[...].astype(F32)).astype(jnp.int32)
    limits[...] = jnp.broadcast_to(counts, (bricks, plane))
    owner_row = owner_ref[...].astype(F32)
    owner_col = column(owner_row)
    square = (bricks, bricks)
    earlier = lax.broadcasted_iota(jnp.int32, square, 1) < lax.broadcasted_iota(jnp.int32, square, 0)
    same = (owner_col == owner_row) & earlier
    rank = jnp.sum(jnp.where(same, 1.0, 0.0), axis=1, keepdims=True)
    destination = owner_col * capacity + rank
    later = lax.broadcasted_iota(jnp.int32, square, 1) > lax.broadcasted_iota(jnp.int32, square, 0)
    before = jnp.where((owner_col == owner_row) & later, 1.0, 0.0)
    destination_row = owner_row * capacity + jnp.sum(before, axis=0, keepdims=True)
    me = lax.axis_index("space")
    slot = lax.broadcasted_iota(jnp.int32, (capacity, bricks), 0)
    picks = []
    for distance in range(spaces):
        goal = (slot + (me + distance) % spaces * capacity).astype(F32)
        picks.append(jnp.where(goal == destination_row, 1.0, 0.0).astype(BF16))

    place = lax.axis_index("tm")
    places = lax.axis_size("tm")
    first_step = place * steps
    odd = place % 2 == 1
    weights = [spline_weights(phase_ref[:, s : s + 1]) for s in range(steps)]
    factors = {}
    for s in range(steps):
        for position in range(-1, steps + 2):
            basis = None
            for j in range(4):
                reach = s - 1 + j
                if position not in (reach, max(reach, 0), min(reach, steps - 1)):
                    continue
                goal = jnp.clip(first_step + reach, 0, places * steps - 1) - first_step
                term = jnp.where(goal == position, weights[s][j], 0.0)
                basis = term if basis is None else basis + term
            if basis is not None:
                factors[position, s] = jnp.where(lane < GRAD_AT, basis * basis, basis)

    def coefficient(position):
        return [
            sum(
                factors[position, s] * moments[s, :, half * LANES : (half + 1) * LANES]
                for s in range(steps)
                if (position, s) in factors
            )
            for half in range(2)
        ]

    for k in range(len(parts)):
        for copy in copies(k):
            copy.wait()
        fill(k, buffers[k % 2])
        reduce(k, buffers[k % 2])

    doubled = (comps + 1) // 2 * NODES
    for s in range(steps):
        halves = [jnp.zeros((bricks, LANES), F32) for _ in range(2)]
        for i in range(groups):
            at = i * rows + s * bricks
            block = sums[at : at + bricks]
            if i < len(pairs):
                half, goal, span = pair_place(i)
                keep = (lane >= goal) & (lane < goal + span)
            else:
                half, goal, span = gradient_place(i - len(pairs))
                keep = (lane >= goal) & (lane < goal + span)
                keep |= (lane >= goal + doubled) & (lane < goal + doubled + span)
            halves[half] = jnp.where(keep, block, halves[half])
        for half in range(2):
            low = pltpu.roll(halves[half], LANES - doubled, 1)
            whole = halves[half] + jnp.where(lane >= GRAD_AT, low, 0.0)
            moments[s, :, half * LANES : (half + 1) * LANES] = whole

    packed_groups, pieces = packing(steps, comps)

    def pack(slabs):
        packed = [jnp.zeros((bricks, LANES), F32) for _ in range(packed_groups)]
        for k, half, source, group, goal, count in pieces:
            if slabs[k] is None:
                continue
            block = slabs[k][half]
            if goal != source:
                block = pltpu.roll(block, (goal - source) % LANES, 1)
            keep = (lane >= goal) & (lane < goal + count)
            packed[group] = jnp.where(keep, block, packed[group])
        return packed

    above = pack([coefficient(steps + k) if k < 2 else None for k in range(steps)])
    below = pack([coefficient(-1) if k == steps - 1 else None for k in range(steps)])
    for group in range(packed_groups):
        cols = slice(group * LANES, (group + 1) * LANES)
        parts_b = split(jnp.where(odd, above[group], below[group]))
        for pick, ref in zip(picks, send_b_refs):
            ref[:, cols] = sum(jnp.dot(pick, part, preferred_element_type=F32) for part in parts_b)
        send_a_ref[:, cols] = jnp.where(odd, below[group], above[group])
    mine = pack([coefficient(k) for k in range(steps)])
    mine[-1] = jnp.where(lane == LANES - 1, destination, mine[-1])
    for group in range(packed_groups):
        own_ref[:, group * LANES : (group + 1) * LANES] = mine[group]


def split(x):
    high = x.astype(BF16)
    return high, (x - high.astype(F32)).astype(BF16)


def place_kernel(capacity, *refs):
    *blocks, out_ref = refs
    me = lax.axis_index("space")
    width = out_ref.shape[1]
    for distance, block in enumerate(blocks):
        slot = lax.broadcasted_iota(jnp.int32, (block.shape[0], capacity), 1)
        goal = (slot + me * capacity).astype(F32)
        pick = jnp.where(goal == block[:, width - 1 :], 1.0, 0.0).astype(BF16)
        out_ref[distance * capacity : (distance + 1) * capacity] = sum(
            lax.dot_general(pick, part, (((0,), (0,)), ((), ())), preferred_element_type=F32)
            for part in split(block[...])
        )


def expand_kernel(
    capacity, ready, last, table, gradient_table, hessian_hbm, gradient_hbm, total, wide, thin, sems
):
    steps, slots, _ = wide.shape
    dofs = thin.shape[1]
    spaces = slots // capacity
    me = lax.axis_index("space")
    for distance in range(spaces):
        here = slice(distance * capacity, (distance + 1) * capacity)
        source = (me + spaces - distance) % spaces
        rows = pl.ds(pl.multiple_of(source * capacity, math.gcd(capacity, 8)), capacity)
        total[rows] = ready[here] + last[here]
    parts = split(total[...])
    copies = []
    for k in range(steps):
        wide[k] = sum(jnp.dot(part, table[k], preferred_element_type=F32) for part in parts)
        copies.append(pltpu.make_async_copy(wide.at[k], hessian_hbm.at[k], sems.at[k]))
        copies[-1].start()
    gradient = sum(
        lax.dot_general(gradient_table[...], part, (((1,), (1,)), ((), ())), preferred_element_type=F32)
        for part in parts
    )
    for k in range(steps):
        thin[k] = gradient[k * dofs : (k + 1) * dofs]
    copies.append(pltpu.make_async_copy(thin, gradient_hbm, sems.at[steps]))
    copies[-1].start()
    for copy in copies:
        copy.wait()


def per_device(image_gradient, residual, phase, counts, owner):
    steps, bricks, comps, voxels = image_gradient.shape
    spaces = lax.axis_size("space")
    places = lax.axis_size("tm")
    capacity = 3 * bricks // (2 * spaces)
    dofs = NODES * comps
    groups = len(component_pairs(comps)) + comps
    parts = voxel_parts(voxels, (2, 6, 8))
    widest = max(width for _, width in parts)
    table, scale = voxel_tables(voxels)
    block = (bricks, packing(steps, comps)[0] * LANES)
    in_hbm = pl.BlockSpec(memory_space=pltpu.HBM)
    own, send_a, *send_b = pl.pallas_call(
        functools.partial(moments_kernel, capacity, parts),
        in_specs=[in_hbm] * 7,
        out_shape=[pltpu.VMEM(block, F32)] * 2 + [pltpu.VMEM((capacity, block[1]), F32)] * spaces,
        scratch_shapes=[
            pltpu.VMEM((steps, comps, bricks, voxels), BF16),
            pltpu.VMEM((steps, bricks, voxels), BF16),
            pltpu.VMEM((1, bricks), jnp.int32),
            pltpu.VMEM((1, bricks), jnp.int32),
            pltpu.VMEM((1, steps), F32),
            pltpu.VMEM((voxels, LANES), BF16),
            pltpu.VMEM(scale.shape, BF16),
            pltpu.VMEM((groups * steps * bricks, widest), BF16),
            pltpu.VMEM((groups * steps * bricks, widest), BF16),
            pltpu.VMEM((bricks, round(voxels ** (2 / 3))), jnp.int32),
            pltpu.VMEM((groups * steps * bricks, LANES), F32),
            pltpu.VMEM((steps, bricks, 2 * LANES), F32),
            pltpu.SemaphoreType.DMA((4,)),
            pltpu.SemaphoreType.DMA((len(parts), 3)),
        ],
        compiler_params=pltpu.CompilerParams(vmem_limit_bytes=32 << 20),
        name="moments",
    )(
        *(
            pltpu.with_memory_space_constraint(x, pltpu.HBM)
            for x in (
                jnp.transpose(image_gradient, (0, 2, 1, 3)),
                residual,
                counts.reshape(1, bricks),
                owner.reshape(1, bricks),
                phase.reshape(1, steps),
                jnp.asarray(table),
                jnp.asarray(scale),
            )
        )
    )

    def exchange(values, start):
        lower = range(start, places - 1, 2)
        route = [(i, i + 1) for i in lower] + [(i + 1, i) for i in lower]
        return lax.ppermute(values, "tm", route) if route else jnp.zeros_like(values)

    def turned(values, distance):
        route = [(i, (i + distance) % spaces) for i in range(spaces)]
        return lax.ppermute(values, "space", route) if distance else values

    for_far = jnp.concatenate([turned(x, distance) for distance, x in enumerate(send_b)])
    near = own + exchange(send_a, 0)
    last = exchange(for_far, 1)
    blocks = [turned(near, distance) for distance in range(spaces)]
    slots = spaces * capacity
    ready = pl.pallas_call(
        functools.partial(place_kernel, capacity),
        out_shape=pltpu.VMEM((slots, block[1]), F32),
        compiler_params=pltpu.CompilerParams(vmem_limit_bytes=8 << 20),
        name="place",
    )(*blocks)
    hessian_table, gradient_table = (jnp.asarray(x) for x in expansion_tables(steps, comps))
    wide = (steps, slots, dofs * dofs)
    thin = (steps, dofs, slots)
    hessian, gradient = pl.pallas_call(
        functools.partial(expand_kernel, capacity),
        out_shape=[jax.ShapeDtypeStruct(wide, F32), jax.ShapeDtypeStruct(thin, F32)],
        out_specs=[in_hbm] * 2,
        scratch_shapes=[
            pltpu.VMEM((slots, block[1]), F32),
            pltpu.VMEM(wide, F32),
            pltpu.VMEM(thin, F32),
            pltpu.SemaphoreType.DMA((steps + 1,)),
        ],
        compiler_params=pltpu.CompilerParams(vmem_limit_bytes=16 << 20),
        name="expand",
    )(ready, last, hessian_table, gradient_table)
    return hessian, jnp.transpose(gradient, (0, 2, 1))


def solution(mesh):
    in_specs = (
        P("tm", "space", None, None),
        P("tm", "space", None),
        P("tm"),
        P("space"),
        P("space", None),
    )
    out_specs = (P("tm", "space", None), P("tm", "space", None))
    return jax.shard_map(
        per_device, mesh=mesh, in_specs=in_specs, out_specs=out_specs, check_vma=False
    )
```

```python
import functools
import math

import ml_dtypes
import numpy as np
import jax
import jax.numpy as jnp
from jax import lax
from jax.experimental import pallas as pl
from jax.experimental.pallas import tpu as pltpu
from jax.sharding import PartitionSpec as P

LANES = 128
QUADS = 27
NODES = 8
PER_HALF = 3
GRAD_AT = PER_HALF * QUADS
BF16 = jnp.bfloat16
F32 = jnp.float32


def component_pairs(comps):
    return [(c, e) for c in range(comps) for e in range(c, comps)]


@functools.cache
def voxel_tables(voxels):
    edge = round(voxels ** (1 / 3))
    at = (np.arange(edge) + 0.5) / edge
    lines = np.stack([1 - at, at])
    quads = np.stack([(1 - at) ** 2, at * (1 - at), at * at])
    shapes = np.einsum("ai,bj,ck->abcijk", lines, lines, lines).reshape(NODES, voxels)
    squares = np.einsum("ai,bj,ck->abcijk", quads, quads, quads).reshape(QUADS, voxels)
    scale = (1 + np.floor(128 * np.modf(np.arange(voxels) * 0.6180339887498949)[0]) / 128).reshape(1, voxels)
    squares = (squares / scale).astype(ml_dtypes.bfloat16)
    high = shapes.astype(ml_dtypes.bfloat16)
    low = (shapes - high.astype(np.float64)).astype(ml_dtypes.bfloat16)
    table = np.zeros((LANES, voxels), ml_dtypes.bfloat16)
    rows = np.concatenate([squares] * PER_HALF + [high, high, low, low])
    table[: len(rows)] = rows
    return np.ascontiguousarray(table.T), np.repeat(scale.astype(ml_dtypes.bfloat16), 16, axis=0)


def voxel_parts(voxels, sixteenths):
    ends = np.cumsum((0,) + sixteenths) * (voxels // 16)
    return tuple((int(a), int(b - a)) for a, b in zip(ends, ends[1:]))


def pair_place(i):
    return i // PER_HALF, i % PER_HALF * QUADS, QUADS


def gradient_place(c):
    return c % 2, GRAD_AT + c // 2 * NODES, NODES


@functools.cache
def packing(steps, comps):
    ends = [0, 0]
    places = [pair_place(i) for i in range(len(component_pairs(comps)))]
    for half, at, count in places + [gradient_place(c) for c in range(comps)]:
        ends[half] = max(ends[half], at + count)
    first = LANES - ends[0]
    rest = ends[1] - first
    assert 0 < 2 * rest < LANES
    pieces = []
    for k in range(steps):
        pieces += [
            (k, 0, 0, k, 0, ends[0]),
            (k, 1, 0, k, ends[0], first),
            (k, 1, first, shared_group(steps, k), k % 2 * rest, rest),
        ]
    return steps + (steps + 1) // 2, tuple(pieces)


def shared_group(steps, k):
    return steps + k // 2


def packed_lane(steps, pieces, step, half, lane):
    for s, h, source, group, goal, count in pieces:
        if (s, h) == (step, half) and source <= lane < source + count:
            return (group >= steps) * LANES + goal + lane - source


@functools.cache
def expansion_tables(steps, comps):
    dofs = NODES * comps
    pairs = component_pairs(comps)
    _, pieces = packing(steps, comps)
    hessian = np.zeros((steps, 2 * LANES, dofs * dofs), ml_dtypes.bfloat16)
    gradient = np.zeros((steps, dofs, 2 * LANES), ml_dtypes.bfloat16)
    for k in range(steps):
        for d in range(dofs):
            a, c = divmod(d, comps)
            half, at, _ = gradient_place(c)
            gradient[k, d, packed_lane(steps, pieces, k, half, at + a)] = 1
            for f in range(dofs):
                b, e = divmod(f, comps)
                quad = sum(((a >> n & 1) + (b >> n & 1)) * 3**n for n in range(3))
                half, at, _ = pair_place(pairs.index((min(c, e), max(c, e))))
                hessian[k, packed_lane(steps, pieces, k, half, at + quad), d * dofs + f] = 1
    return hessian, gradient


def spline_weights(phase):
    return [
        (1.0 - phase) ** 3 / 6.0,
        (3.0 * phase**3 - 6.0 * phase**2 + 4.0) / 6.0,
        (-3.0 * phase**3 + 3.0 * phase**2 + 3.0 * phase + 1.0) / 6.0,
        phase**3 / 6.0,
    ]


def column(row):
    n = row.shape[1]
    eye = lax.broadcasted_iota(jnp.int32, (n, n), 0) == lax.broadcasted_iota(jnp.int32, (n, n), 1)
    return jnp.sum(jnp.where(eye, jnp.broadcast_to(row, (n, n)), 0.0), axis=1, keepdims=True)


def moments_kernel(
    capacity,
    parts,
    grads_hbm,
    resid_hbm,
    counts_hbm,
    owner_hbm,
    phase_hbm,
    table_hbm,
    scale_hbm,
    own_ref,
    send_a_ref,
    *refs,
):
    spaces = lax.axis_size("space")
    send_b_refs, refs = refs[:spaces], refs[spaces:]
    (
        grads,
        resid,
        counts_ref,
        owner_ref,
        phase_ref,
        table,
        scale,
        products_a,
        products_b,
        limits,
        sums,
        moments,
        small_sems,
        sems,
    ) = refs
    steps, comps, bricks, voxels = grads.shape
    pairs = component_pairs(comps)
    groups = len(pairs) + comps
    rows = steps * bricks
    plane = round(voxels ** (2 / 3))
    buffers = (products_a, products_b)
    small = [
        pltpu.make_async_copy(src, dst, small_sems.at[i])
        for i, (src, dst) in enumerate(
            [
                (counts_hbm, counts_ref),
                (owner_hbm, owner_ref),
                (phase_hbm, phase_ref),
                (scale_hbm, scale),
            ]
        )
    ]

    def copies(k):
        start, width = parts[k]
        cols = pl.ds(start, width)
        return (
            pltpu.make_async_copy(grads_hbm.at[:, :, :, cols], grads.at[:, :, :, cols], sems.at[k, 0]),
            pltpu.make_async_copy(resid_hbm.at[:, :, cols], resid.at[:, :, cols], sems.at[k, 1]),
            pltpu.make_async_copy(table_hbm.at[cols], table.at[cols], sems.at[k, 2]),
        )

    for copy in small:
        copy.start()
    for k in range(len(parts)):
        for copy in copies(k):
            copy.start(priority=min(k, 1))

    lane = lax.broadcasted_iota(jnp.int32, (1, LANES), 1)
    tall = math.gcd(bricks, 16)
    voxel = lax.broadcasted_iota(jnp.int16, (tall, plane), 1)
    zero = jnp.zeros((), BF16)

    def fill(k, products):
        start, width = parts[k]
        for b in range(0, bricks, tall):
            limit = (limits[b : b + tall] - start).astype(jnp.int16)
            left = [[None] * comps for _ in range(steps)]
            for p in range(0, width, plane):
                cols = slice(start + p, start + p + plane)
                valid = voxel + jnp.int16(p) < limit
                scale_here = jnp.where(valid, scale[:tall, cols], zero)
                for s in range(steps):
                    resid_here = jnp.where(valid, resid[s, b : b + tall, cols], zero).astype(F32)
                    g = [grads[s, c, b : b + tall, cols] for c in range(comps)]
                    scaled = [x * scale_here for x in g]
                    blocks = [scaled[c] * g[e] for c, e in pairs]
                    for c in range(comps):
                        exact = g[c].astype(F32) * resid_here
                        if left[s][c] is not None:
                            exact = exact + left[s][c]
                        blocks.append(exact.astype(BF16))
                        left[s][c] = exact - blocks[-1].astype(F32)
                    for i, block in enumerate(blocks):
                        at = i * rows + s * bricks + b
                        products[at : at + tall, p : p + plane] = block

    def reduce(k, products):
        start, width = parts[k]
        for at in range(0, groups * rows, groups * rows // 2):
            here = slice(at, at + groups * rows // 2)
            part = jnp.dot(products[here, :width], table[start : start + width], preferred_element_type=F32)
            sums[here] = part if k == 0 else sums[here] + part

    for copy in small:
        copy.wait()
    counts = column(counts_ref[...].astype(F32)).astype(jnp.int32)
    limits[...] = jnp.broadcast_to(counts, (bricks, plane))
    owner_row = owner_ref[...].astype(F32)
    owner_col = column(owner_row)
    square = (bricks, bricks)
    earlier = lax.broadcasted_iota(jnp.int32, square, 1) < lax.broadcasted_iota(jnp.int32, square, 0)
    same = (owner_col == owner_row) & earlier
    rank = jnp.sum(jnp.where(same, 1.0, 0.0), axis=1, keepdims=True)
    destination = owner_col * capacity + rank
    later = lax.broadcasted_iota(jnp.int32, square, 1) > lax.broadcasted_iota(jnp.int32, square, 0)
    before = jnp.where((owner_col == owner_row) & later, 1.0, 0.0)
    destination_row = owner_row * capacity + jnp.sum(before, axis=0, keepdims=True)
    me = lax.axis_index("space")
    slot = lax.broadcasted_iota(jnp.int32, (capacity, bricks), 0)
    picks = []
    for distance in range(spaces):
        goal = (slot + (me + distance) % spaces * capacity).astype(F32)
        picks.append(jnp.where(goal == destination_row, 1.0, 0.0).astype(BF16))

    place = lax.axis_index("tm")
    places = lax.axis_size("tm")
    first_step = place * steps
    odd = place % 2 == 1
    weights = [spline_weights(phase_ref[:, s : s + 1]) for s in range(steps)]
    factors = {}
    for s in range(steps):
        for position in range(-1, steps + 2):
            basis = None
            for j in range(4):
                reach = s - 1 + j
                if position not in (reach, max(reach, 0), min(reach, steps - 1)):
                    continue
                goal = jnp.clip(first_step + reach, 0, places * steps - 1) - first_step
                term = jnp.where(goal == position, weights[s][j], 0.0)
                basis = term if basis is None else basis + term
            if basis is not None:
                factors[position, s] = jnp.where(lane < GRAD_AT, basis * basis, basis)

    def coefficient(position):
        return [
            sum(
                factors[position, s] * moments[s, :, half * LANES : (half + 1) * LANES]
                for s in range(steps)
                if (position, s) in factors
            )
            for half in range(2)
        ]

    for k in range(len(parts)):
        for copy in copies(k):
            copy.wait()
        fill(k, buffers[k % 2])
        reduce(k, buffers[k % 2])

    doubled = (comps + 1) // 2 * NODES
    for s in range(steps):
        halves = [jnp.zeros((bricks, LANES), F32) for _ in range(2)]
        for i in range(groups):
            at = i * rows + s * bricks
            block = sums[at : at + bricks]
            if i < len(pairs):
                half, goal, span = pair_place(i)
                keep = (lane >= goal) & (lane < goal + span)
            else:
                half, goal, span = gradient_place(i - len(pairs))
                keep = (lane >= goal) & (lane < goal + span)
                keep |= (lane >= goal + doubled) & (lane < goal + doubled + span)
            halves[half] = jnp.where(keep, block, halves[half])
        for half in range(2):
            low = pltpu.roll(halves[half], LANES - doubled, 1)
            whole = halves[half] + jnp.where(lane >= GRAD_AT, low, 0.0)
            moments[s, :, half * LANES : (half + 1) * LANES] = whole

    packed_groups, pieces = packing(steps, comps)

    def pack(slabs):
        packed = [jnp.zeros((bricks, LANES), F32) for _ in range(packed_groups)]
        for k, half, source, group, goal, count in pieces:
            if slabs[k] is None:
                continue
            block = slabs[k][half]
            if goal != source:
                block = pltpu.roll(block, (goal - source) % LANES, 1)
            keep = (lane >= goal) & (lane < goal + count)
            packed[group] = jnp.where(keep, block, packed[group])
        return packed

    above = pack([coefficient(steps + k) if k < 2 else None for k in range(steps)])
    below = pack([coefficient(-1) if k == steps - 1 else None for k in range(steps)])
    for group in range(packed_groups):
        cols = slice(group * LANES, (group + 1) * LANES)
        parts_b = split(jnp.where(odd, above[group], below[group]))
        for pick, ref in zip(picks, send_b_refs):
            ref[:, cols] = sum(jnp.dot(pick, part, preferred_element_type=F32) for part in parts_b)
        send_a_ref[:, cols] = jnp.where(odd, below[group], above[group])
    mine = pack([coefficient(k) for k in range(steps)])
    mine[-1] = jnp.where(lane == LANES - 1, destination, mine[-1])
    for group in range(packed_groups):
        own_ref[:, group * LANES : (group + 1) * LANES] = mine[group]


def split(x):
    high = x.astype(BF16)
    return high, (x - high.astype(F32)).astype(BF16)


def place_kernel(capacity, *refs):
    *blocks, out_ref = refs
    me = lax.axis_index("space")
    width = out_ref.shape[1]
    for distance, block in enumerate(blocks):
        slot = lax.broadcasted_iota(jnp.int32, (block.shape[0], capacity), 1)
        goal = (slot + me * capacity).astype(F32)
        pick = jnp.where(goal == block[:, width - 1 :], 1.0, 0.0).astype(BF16)
        out_ref[distance * capacity : (distance + 1) * capacity] = sum(
            lax.dot_general(pick, part, (((0,), (0,)), ((), ())), preferred_element_type=F32)
            for part in split(block[...])
        )


def expand_kernel(
    capacity, ready, last, table, gradient_table, hessian_hbm, gradient_hbm, total, wide, thin, sems
):
    steps, slots, _ = wide.shape
    spaces = slots // capacity
    me = lax.axis_index("space")
    for distance in range(spaces):
        here = slice(distance * capacity, (distance + 1) * capacity)
        source = (me + spaces - distance) % spaces
        rows = pl.ds(pl.multiple_of(source * capacity, math.gcd(capacity, 8)), capacity)
        total[rows] = ready[here] + last[here]
    copies = []
    parts = []
    for k in range(steps):
        lanes = [slice(g * LANES, (g + 1) * LANES) for g in (k, shared_group(steps, k))]
        parts.append(split(jnp.concatenate([total[:, cols] for cols in lanes], axis=1)))
        wide[k] = sum(jnp.dot(part, table[k], preferred_element_type=F32) for part in parts[k])
        copies.append(pltpu.make_async_copy(wide.at[k], hessian_hbm.at[k], sems.at[k]))
        copies[-1].start()
    for k in range(steps):
        thin[k] = sum(
            lax.dot_general(gradient_table[k], part, (((1,), (1,)), ((), ())), preferred_element_type=F32)
            for part in parts[k]
        )
    copies.append(pltpu.make_async_copy(thin, gradient_hbm, sems.at[steps]))
    copies[-1].start()
    for copy in copies:
        copy.wait()


def per_device(image_gradient, residual, phase, counts, owner):
    steps, bricks, comps, voxels = image_gradient.shape
    spaces = lax.axis_size("space")
    places = lax.axis_size("tm")
    capacity = 3 * bricks // (2 * spaces)
    dofs = NODES * comps
    groups = len(component_pairs(comps)) + comps
    parts = voxel_parts(voxels, (2, 6, 8))
    widest = max(width for _, width in parts)
    table, scale = voxel_tables(voxels)
    block = (bricks, packing(steps, comps)[0] * LANES)
    in_hbm = pl.BlockSpec(memory_space=pltpu.HBM)
    own, send_a, *send_b = pl.pallas_call(
        functools.partial(moments_kernel, capacity, parts),
        in_specs=[in_hbm] * 7,
        out_shape=[pltpu.VMEM(block, F32)] * 2 + [pltpu.VMEM((capacity, block[1]), F32)] * spaces,
        scratch_shapes=[
            pltpu.VMEM((steps, comps, bricks, voxels), BF16),
            pltpu.VMEM((steps, bricks, voxels), BF16),
            pltpu.VMEM((1, bricks), jnp.int32),
            pltpu.VMEM((1, bricks), jnp.int32),
            pltpu.VMEM((1, steps), F32),
            pltpu.VMEM((voxels, LANES), BF16),
            pltpu.VMEM(scale.shape, BF16),
            pltpu.VMEM((groups * steps * bricks, widest), BF16),
            pltpu.VMEM((groups * steps * bricks, widest), BF16),
            pltpu.VMEM((bricks, round(voxels ** (2 / 3))), jnp.int32),
            pltpu.VMEM((groups * steps * bricks, LANES), F32),
            pltpu.VMEM((steps, bricks, 2 * LANES), F32),
            pltpu.SemaphoreType.DMA((4,)),
            pltpu.SemaphoreType.DMA((len(parts), 3)),
        ],
        compiler_params=pltpu.CompilerParams(vmem_limit_bytes=32 << 20),
        name="moments",
    )(
        *(
            pltpu.with_memory_space_constraint(x, pltpu.HBM)
            for x in (
                jnp.transpose(image_gradient, (0, 2, 1, 3)),
                residual,
                counts.reshape(1, bricks),
                owner.reshape(1, bricks),
                phase.reshape(1, steps),
                jnp.asarray(table),
                jnp.asarray(scale),
            )
        )
    )

    def exchange(values, start):
        lower = range(start, places - 1, 2)
        route = [(i, i + 1) for i in lower] + [(i + 1, i) for i in lower]
        return lax.ppermute(values, "tm", route) if route else jnp.zeros_like(values)

    def turned(values, distance):
        route = [(i, (i + distance) % spaces) for i in range(spaces)]
        return lax.ppermute(values, "space", route) if distance else values

    for_far = jnp.concatenate([turned(x, distance) for distance, x in enumerate(send_b)])
    near = own + exchange(send_a, 0)
    last = exchange(for_far, 1)
    blocks = [turned(near, distance) for distance in range(spaces)]
    slots = spaces * capacity
    ready = pl.pallas_call(
        functools.partial(place_kernel, capacity),
        out_shape=pltpu.VMEM((slots, block[1]), F32),
        compiler_params=pltpu.CompilerParams(vmem_limit_bytes=8 << 20),
        name="place",
    )(*blocks)
    hessian_table, gradient_table = (jnp.asarray(x) for x in expansion_tables(steps, comps))
    wide = (steps, slots, dofs * dofs)
    thin = (steps, dofs, slots)
    hessian, gradient = pl.pallas_call(
        functools.partial(expand_kernel, capacity),
        out_shape=[jax.ShapeDtypeStruct(wide, F32), jax.ShapeDtypeStruct(thin, F32)],
        out_specs=[in_hbm] * 2,
        scratch_shapes=[
            pltpu.VMEM((slots, block[1]), F32),
            pltpu.VMEM(wide, F32),
            pltpu.VMEM(thin, F32),
            pltpu.SemaphoreType.DMA((steps + 1,)),
        ],
        compiler_params=pltpu.CompilerParams(vmem_limit_bytes=16 << 20),
        name="expand",
    )(ready, last, hessian_table, gradient_table)
    return hessian, jnp.transpose(gradient, (0, 2, 1))


def solution(mesh):
    in_specs = (
        P("tm", "space", None, None),
        P("tm", "space", None),
        P("tm"),
        P("space"),
        P("space", None),
    )
    out_specs = (P("tm", "space", None), P("tm", "space", None))
    return jax.shard_map(
        per_device, mesh=mesh, in_specs=in_specs, out_specs=out_specs, check_vma=False
    )
```

```python
import functools
import math

import ml_dtypes
import numpy as np
import jax
import jax.numpy as jnp
from jax import lax
from jax.experimental import pallas as pl
from jax.experimental.pallas import tpu as pltpu
from jax.sharding import PartitionSpec as P

LANES = 128
QUADS = 27
NODES = 8
PER_HALF = 3
GRAD_AT = PER_HALF * QUADS
BF16 = jnp.bfloat16
F32 = jnp.float32


def component_pairs(comps):
    return [(c, e) for c in range(comps) for e in range(c, comps)]


@functools.cache
def voxel_tables(voxels, comps):
    edge = round(voxels ** (1 / 3))
    at = (np.arange(edge) + 0.5) / edge
    quads = np.stack([(1 - at) ** 2, at * (1 - at), at * at])
    odds = 2 * np.arange(edge) + 1 - edge
    across = np.stack([odds[:, None] ** (m >> 1) * odds[None, :] ** (m & 1) for m in range(4)]).reshape(4, edge * edge)
    squares = np.einsum("ai,bj,ck->abcijk", quads, quads, quads).reshape(QUADS, voxels)
    scale = (1 + np.floor(128 * np.modf(np.arange(voxels) * 0.6180339887498949)[0]) / 128).reshape(1, voxels)
    squares = (squares / scale).astype(ml_dtypes.bfloat16)
    table = np.zeros((voxels, LANES), ml_dtypes.bfloat16)
    table[:, :GRAD_AT] = np.concatenate([squares] * PER_HALF).T
    plane_table = np.zeros((edge * edge, LANES), ml_dtypes.bfloat16)
    lines = np.concatenate([across] * (2 * ((comps + 1) // 2)))
    plane_table[:, GRAD_AT : GRAD_AT + len(lines)] = lines.T
    return table, plane_table, np.repeat(scale.astype(ml_dtypes.bfloat16), 16, axis=0)


def voxel_parts(voxels, sixteenths):
    ends = np.cumsum((0,) + sixteenths) * (voxels // 16)
    return tuple((int(a), int(b - a)) for a, b in zip(ends, ends[1:]))


def pair_place(i):
    return i // PER_HALF, i % PER_HALF * QUADS, QUADS


def gradient_place(c):
    return c % 2, GRAD_AT + c // 2 * NODES, NODES


@functools.cache
def packing(steps, comps):
    ends = [0, 0]
    places = [pair_place(i) for i in range(len(component_pairs(comps)))]
    for half, at, count in places + [gradient_place(c) for c in range(comps)]:
        ends[half] = max(ends[half], at + count)
    first = LANES - ends[0]
    rest = ends[1] - first
    assert 0 < 2 * rest < LANES
    pieces = []
    for k in range(steps):
        pieces += [
            (k, 0, 0, k, 0, ends[0]),
            (k, 1, 0, k, ends[0], first),
            (k, 1, first, shared_group(steps, k), k % 2 * rest, rest),
        ]
    return steps + (steps + 1) // 2, tuple(pieces)


def shared_group(steps, k):
    return steps + k // 2


def packed_lane(steps, pieces, step, half, lane):
    for s, h, source, group, goal, count in pieces:
        if (s, h) == (step, half) and source <= lane < source + count:
            return (group >= steps) * LANES + goal + lane - source


@functools.cache
def expansion_tables(steps, comps, edge):
    dofs = NODES * comps
    pairs = component_pairs(comps)
    _, pieces = packing(steps, comps)
    hessian = np.zeros((steps, 2 * LANES, dofs * dofs), ml_dtypes.bfloat16)
    gradient = np.zeros((steps, dofs, 2 * LANES), ml_dtypes.bfloat16)
    for k in range(steps):
        for d in range(dofs):
            a, c = divmod(d, comps)
            half, at, _ = gradient_place(c)
            for m in range(4):
                weight = 0.25
                for bit in range(2):
                    if m >> bit & 1:
                        weight *= (1 if a >> bit & 1 else -1) / edge
                lane = packed_lane(steps, pieces, k, half, at + (a >> 2) * 4 + m)
                gradient[k, d, lane] = weight
            for f in range(dofs):
                b, e = divmod(f, comps)
                quad = sum(((a >> n & 1) + (b >> n & 1)) * 3**n for n in range(3))
                half, at, _ = pair_place(pairs.index((min(c, e), max(c, e))))
                hessian[k, packed_lane(steps, pieces, k, half, at + quad), d * dofs + f] = 1
    return hessian, gradient


def spline_weights(phase):
    return [
        (1.0 - phase) ** 3 / 6.0,
        (3.0 * phase**3 - 6.0 * phase**2 + 4.0) / 6.0,
        (-3.0 * phase**3 + 3.0 * phase**2 + 3.0 * phase + 1.0) / 6.0,
        phase**3 / 6.0,
    ]


def column(row):
    n = row.shape[1]
    eye = lax.broadcasted_iota(jnp.int32, (n, n), 0) == lax.broadcasted_iota(jnp.int32, (n, n), 1)
    return jnp.sum(jnp.where(eye, jnp.broadcast_to(row, (n, n)), 0.0), axis=1, keepdims=True)


def moments_kernel(
    capacity,
    parts,
    grads_hbm,
    resid_hbm,
    counts_hbm,
    owner_hbm,
    phase_hbm,
    table_hbm,
    plane_table_hbm,
    scale_hbm,
    own_ref,
    send_a_ref,
    *refs,
):
    spaces = lax.axis_size("space")
    send_b_refs, refs = refs[:spaces], refs[spaces:]
    (
        grads,
        resid,
        counts_ref,
        owner_ref,
        phase_ref,
        table,
        plane_table,
        scale,
        products_a,
        products_b,
        limits,
        running,
        lines,
        sums,
        moments,
        small_sems,
        sems,
    ) = refs
    steps, comps, bricks, voxels = grads.shape
    pairs = component_pairs(comps)
    groups = len(pairs)
    rows = steps * bricks
    plane = round(voxels ** (2 / 3))
    buffers = (products_a, products_b)
    small = [
        pltpu.make_async_copy(src, dst, small_sems.at[i])
        for i, (src, dst) in enumerate(
            [
                (counts_hbm, counts_ref),
                (owner_hbm, owner_ref),
                (phase_hbm, phase_ref),
                (scale_hbm, scale),
                (plane_table_hbm, plane_table),
            ]
        )
    ]

    def copies(k):
        start, width = parts[k]
        cols = pl.ds(start, width)
        return (
            pltpu.make_async_copy(grads_hbm.at[:, :, :, cols], grads.at[:, :, :, cols], sems.at[k, 0]),
            pltpu.make_async_copy(resid_hbm.at[:, :, cols], resid.at[:, :, cols], sems.at[k, 1]),
            pltpu.make_async_copy(table_hbm.at[cols], table.at[cols], sems.at[k, 2]),
        )

    for copy in small:
        copy.start()
    for k in range(len(parts)):
        for copy in copies(k):
            copy.start(priority=min(k, 1))

    lane = lax.broadcasted_iota(jnp.int32, (1, LANES), 1)
    tall = math.gcd(bricks, 16)
    voxel = lax.broadcasted_iota(jnp.int16, (tall, plane), 1)
    zero = jnp.zeros((), BF16)

    edge = voxels // plane

    def fill(k, products):
        start, width = parts[k]
        for b in range(0, bricks, tall):
            limit = (limits[b : b + tall] - start).astype(jnp.int16)
            for s in range(steps):
                total = [running[0, c, s, b : b + tall] for c in range(comps)] if k else None
                ramp = [running[1, c, s, b : b + tall] for c in range(comps)] if k else None
                for p in range(0, width, plane):
                    cols = slice(start + p, start + p + plane)
                    valid = voxel + jnp.int16(p) < limit
                    scale_here = jnp.where(valid, scale[:tall, cols], zero)
                    resid_here = jnp.where(valid, resid[s, b : b + tall, cols], zero).astype(F32)
                    g = [grads[s, c, b : b + tall, cols] for c in range(comps)]
                    scaled = [x * scale_here for x in g]
                    for i, (c, e) in enumerate(pairs):
                        at = i * rows + s * bricks + b
                        products[at : at + tall, p : p + plane] = scaled[c] * g[e]
                    terms = [x.astype(F32) * resid_here for x in g]
                    total = terms if total is None else [x + y for x, y in zip(total, terms)]
                    ramp = total if ramp is None else [x + y for x, y in zip(ramp, total)]
                for c in range(comps):
                    if k + 1 < len(parts):
                        running[0, c, s, b : b + tall] = total[c]
                        running[1, c, s, b : b + tall] = ramp[c]
                        continue
                    falling = (ramp[c] - 0.5 * total[c]) * (1.0 / edge)
                    for n, line in enumerate((falling, total[c] - falling)):
                        at = ((n * comps + c) * steps + s) * bricks + b
                        for m, part in enumerate(split(line)):
                            lines[m, at : at + tall] = part

    def reduce(k, products):
        start, width = parts[k]
        for at in range(0, groups * rows, groups * rows // 2):
            here = slice(at, at + groups * rows // 2)
            part = jnp.dot(products[here, :width], table[start : start + width], preferred_element_type=F32)
            sums[here] = part if k == 0 else sums[here] + part

    for copy in small:
        copy.wait()
    counts = column(counts_ref[...].astype(F32)).astype(jnp.int32)
    limits[...] = jnp.broadcast_to(counts, (bricks, plane))
    owner_row = owner_ref[...].astype(F32)
    owner_col = column(owner_row)
    square = (bricks, bricks)
    earlier = lax.broadcasted_iota(jnp.int32, square, 1) < lax.broadcasted_iota(jnp.int32, square, 0)
    same = (owner_col == owner_row) & earlier
    rank = jnp.sum(jnp.where(same, 1.0, 0.0), axis=1, keepdims=True)
    destination = owner_col * capacity + rank
    later = lax.broadcasted_iota(jnp.int32, square, 1) > lax.broadcasted_iota(jnp.int32, square, 0)
    before = jnp.where((owner_col == owner_row) & later, 1.0, 0.0)
    destination_row = owner_row * capacity + jnp.sum(before, axis=0, keepdims=True)
    me = lax.axis_index("space")
    slot = lax.broadcasted_iota(jnp.int32, (capacity, bricks), 0)
    picks = []
    for distance in range(spaces):
        goal = (slot + (me + distance) % spaces * capacity).astype(F32)
        picks.append(jnp.where(goal == destination_row, 1.0, 0.0).astype(BF16))

    place = lax.axis_index("tm")
    places = lax.axis_size("tm")
    first_step = place * steps
    odd = place % 2 == 1
    weights = [spline_weights(phase_ref[:, s : s + 1]) for s in range(steps)]
    factors = {}
    for s in range(steps):
        for position in range(-1, steps + 2):
            basis = None
            for j in range(4):
                reach = s - 1 + j
                if position not in (reach, max(reach, 0), min(reach, steps - 1)):
                    continue
                goal = jnp.clip(first_step + reach, 0, places * steps - 1) - first_step
                term = jnp.where(goal == position, weights[s][j], 0.0)
                basis = term if basis is None else basis + term
            if basis is not None:
                factors[position, s] = jnp.where(lane < GRAD_AT, basis * basis, basis)

    def coefficient(position):
        return [
            sum(
                factors[position, s] * moments[s, :, half * LANES : (half + 1) * LANES]
                for s in range(steps)
                if (position, s) in factors
            )
            for half in range(2)
        ]

    for k in range(len(parts)):
        for copy in copies(k):
            copy.wait()
        fill(k, buffers[k % 2])
        reduce(k, buffers[k % 2])

    line_sums = sum(
        jnp.dot(lines[m], plane_table[...], preferred_element_type=F32) for m in range(2)
    )
    for s in range(steps):
        halves = [jnp.zeros((bricks, LANES), F32) for _ in range(2)]
        for i in range(len(pairs)):
            half, goal, span = pair_place(i)
            at = i * rows + s * bricks
            keep = (lane >= goal) & (lane < goal + span)
            halves[half] = jnp.where(keep, sums[at : at + bricks], halves[half])
        for c in range(comps):
            half, goal, span = gradient_place(c)
            for n in range(2):
                at = (n * comps + c) * rows + s * bricks
                first = goal + n * span // 2
                keep = (lane >= first) & (lane < first + span // 2)
                halves[half] = jnp.where(keep, line_sums[at : at + bricks], halves[half])
        for half in range(2):
            moments[s, :, half * LANES : (half + 1) * LANES] = halves[half]

    packed_groups, pieces = packing(steps, comps)

    def pack(slabs):
        packed = [jnp.zeros((bricks, LANES), F32) for _ in range(packed_groups)]
        for k, half, source, group, goal, count in pieces:
            if slabs[k] is None:
                continue
            block = slabs[k][half]
            if goal != source:
                block = pltpu.roll(block, (goal - source) % LANES, 1)
            keep = (lane >= goal) & (lane < goal + count)
            packed[group] = jnp.where(keep, block, packed[group])
        return packed

    above = pack([coefficient(steps + k) if k < 2 else None for k in range(steps)])
    below = pack([coefficient(-1) if k == steps - 1 else None for k in range(steps)])
    for group in range(packed_groups):
        cols = slice(group * LANES, (group + 1) * LANES)
        parts_b = split(jnp.where(odd, above[group], below[group]))
        for pick, ref in zip(picks, send_b_refs):
            ref[:, cols] = sum(jnp.dot(pick, part, preferred_element_type=F32) for part in parts_b)
        send_a_ref[:, cols] = jnp.where(odd, below[group], above[group])
    mine = pack([coefficient(k) for k in range(steps)])
    mine[-1] = jnp.where(lane == LANES - 1, destination, mine[-1])
    for group in range(packed_groups):
        own_ref[:, group * LANES : (group + 1) * LANES] = mine[group]


def split(x):
    high = x.astype(BF16)
    return high, (x - high.astype(F32)).astype(BF16)


def place_kernel(capacity, *refs):
    *blocks, out_ref = refs
    me = lax.axis_index("space")
    width = out_ref.shape[1]
    for distance, block in enumerate(blocks):
        slot = lax.broadcasted_iota(jnp.int32, (block.shape[0], capacity), 1)
        goal = (slot + me * capacity).astype(F32)
        pick = jnp.where(goal == block[:, width - 1 :], 1.0, 0.0).astype(BF16)
        out_ref[distance * capacity : (distance + 1) * capacity] = sum(
            lax.dot_general(pick, part, (((0,), (0,)), ((), ())), preferred_element_type=F32)
            for part in split(block[...])
        )


def expand_kernel(
    capacity, ready, last, table, gradient_table, hessian_hbm, gradient_hbm, total, wide, thin, sems
):
    steps, slots, _ = wide.shape
    spaces = slots // capacity
    me = lax.axis_index("space")
    for distance in range(spaces):
        here = slice(distance * capacity, (distance + 1) * capacity)
        source = (me + spaces - distance) % spaces
        rows = pl.ds(pl.multiple_of(source * capacity, math.gcd(capacity, 8)), capacity)
        total[rows] = ready[here] + last[here]
    copies = []
    parts = []
    for k in range(steps):
        lanes = [slice(g * LANES, (g + 1) * LANES) for g in (k, shared_group(steps, k))]
        parts.append(split(jnp.concatenate([total[:, cols] for cols in lanes], axis=1)))
        wide[k] = sum(jnp.dot(part, table[k], preferred_element_type=F32) for part in parts[k])
        copies.append(pltpu.make_async_copy(wide.at[k], hessian_hbm.at[k], sems.at[k]))
        copies[-1].start()
    for k in range(steps):
        thin[k] = sum(
            lax.dot_general(gradient_table[k], part, (((1,), (1,)), ((), ())), preferred_element_type=F32)
            for part in parts[k]
        )
    copies.append(pltpu.make_async_copy(thin, gradient_hbm, sems.at[steps]))
    copies[-1].start()
    for copy in copies:
        copy.wait()


def per_device(image_gradient, residual, phase, counts, owner):
    steps, bricks, comps, voxels = image_gradient.shape
    spaces = lax.axis_size("space")
    places = lax.axis_size("tm")
    capacity = 3 * bricks // (2 * spaces)
    dofs = NODES * comps
    groups = len(component_pairs(comps))
    plane = round(voxels ** (2 / 3))
    parts = voxel_parts(voxels, (3, 6, 5, 2))
    widest = max(width for _, width in parts)
    table, plane_table, scale = voxel_tables(voxels, comps)
    block = (bricks, packing(steps, comps)[0] * LANES)
    in_hbm = pl.BlockSpec(memory_space=pltpu.HBM)
    own, send_a, *send_b = pl.pallas_call(
        functools.partial(moments_kernel, capacity, parts),
        in_specs=[in_hbm] * 8,
        out_shape=[pltpu.VMEM(block, F32)] * 2 + [pltpu.VMEM((capacity, block[1]), F32)] * spaces,
        scratch_shapes=[
            pltpu.VMEM((steps, comps, bricks, voxels), BF16),
            pltpu.VMEM((steps, bricks, voxels), BF16),
            pltpu.VMEM((1, bricks), jnp.int32),
            pltpu.VMEM((1, bricks), jnp.int32),
            pltpu.VMEM((1, steps), F32),
            pltpu.VMEM((voxels, LANES), BF16),
            pltpu.VMEM((plane, LANES), BF16),
            pltpu.VMEM(scale.shape, BF16),
            pltpu.VMEM((groups * steps * bricks, widest), BF16),
            pltpu.VMEM((groups * steps * bricks, widest), BF16),
            pltpu.VMEM((bricks, plane), jnp.int32),
            pltpu.VMEM((2, comps, steps, bricks, plane), F32),
            pltpu.VMEM((2, 2 * comps * steps * bricks, plane), BF16),
            pltpu.VMEM((groups * steps * bricks, LANES), F32),
            pltpu.VMEM((steps, bricks, 2 * LANES), F32),
            pltpu.SemaphoreType.DMA((5,)),
            pltpu.SemaphoreType.DMA((len(parts), 3)),
        ],
        compiler_params=pltpu.CompilerParams(vmem_limit_bytes=32 << 20),
        name="moments",
    )(
        *(
            pltpu.with_memory_space_constraint(x, pltpu.HBM)
            for x in (
                jnp.transpose(image_gradient, (0, 2, 1, 3)),
                residual,
                counts.reshape(1, bricks),
                owner.reshape(1, bricks),
                phase.reshape(1, steps),
                jnp.asarray(table),
                jnp.asarray(plane_table),
                jnp.asarray(scale),
            )
        )
    )

    def exchange(values, start):
        lower = range(start, places - 1, 2)
        route = [(i, i + 1) for i in lower] + [(i + 1, i) for i in lower]
        return lax.ppermute(values, "tm", route) if route else jnp.zeros_like(values)

    def turned(values, distance):
        route = [(i, (i + distance) % spaces) for i in range(spaces)]
        return lax.ppermute(values, "space", route) if distance else values

    for_far = jnp.concatenate([turned(x, distance) for distance, x in enumerate(send_b)])
    near = own + exchange(send_a, 0)
    last = exchange(for_far, 1)
    blocks = [turned(near, distance) for distance in range(spaces)]
    slots = spaces * capacity
    ready = pl.pallas_call(
        functools.partial(place_kernel, capacity),
        out_shape=pltpu.VMEM((slots, block[1]), F32),
        compiler_params=pltpu.CompilerParams(vmem_limit_bytes=8 << 20),
        name="place",
    )(*blocks)
    hessian_table, gradient_table = (jnp.asarray(x) for x in expansion_tables(steps, comps, round(voxels ** (1 / 3))))
    wide = (steps, slots, dofs * dofs)
    thin = (steps, dofs, slots)
    hessian, gradient = pl.pallas_call(
        functools.partial(expand_kernel, capacity),
        out_shape=[jax.ShapeDtypeStruct(wide, F32), jax.ShapeDtypeStruct(thin, F32)],
        out_specs=[in_hbm] * 2,
        scratch_shapes=[
            pltpu.VMEM((slots, block[1]), F32),
            pltpu.VMEM(wide, F32),
            pltpu.VMEM(thin, F32),
            pltpu.SemaphoreType.DMA((steps + 1,)),
        ],
        compiler_params=pltpu.CompilerParams(vmem_limit_bytes=16 << 20),
        name="expand",
    )(ready, last, hessian_table, gradient_table)
    return hessian, jnp.transpose(gradient, (0, 2, 1))


def solution(mesh):
    in_specs = (
        P("tm", "space", None, None),
        P("tm", "space", None),
        P("tm"),
        P("space"),
        P("space", None),
    )
    out_specs = (P("tm", "space", None), P("tm", "space", None))
    return jax.shard_map(
        per_device, mesh=mesh, in_specs=in_specs, out_specs=out_specs, check_vma=False
    )
```

```python
import functools
import math

import ml_dtypes
import numpy as np
import jax
import jax.numpy as jnp
from jax import lax
from jax.experimental import pallas as pl
from jax.experimental.pallas import tpu as pltpu
from jax.sharding import PartitionSpec as P

LANES = 128
QUADS = 27
NODES = 8
PER_HALF = 3
GRAD_AT = PER_HALF * QUADS
BF16 = jnp.bfloat16
F32 = jnp.float32


def component_pairs(comps):
    return [(c, e) for c in range(comps) for e in range(c, comps)]


@functools.cache
def voxel_tables(voxels, comps):
    edge = round(voxels ** (1 / 3))
    at = (np.arange(edge) + 0.5) / edge
    quads = np.stack([(1 - at) ** 2, at * (1 - at), at * at])
    odds = 2 * np.arange(edge) + 1 - edge
    across = np.stack([odds[:, None] ** (m >> 1) * odds[None, :] ** (m & 1) for m in range(4)]).reshape(4, edge * edge)
    squares = np.einsum("ai,bj,ck->abcijk", quads, quads, quads).reshape(QUADS, voxels)
    scale = (1 + np.floor(128 * np.modf(np.arange(voxels) * 0.6180339887498949)[0]) / 128).reshape(1, voxels)
    squares = (squares / scale).astype(ml_dtypes.bfloat16)
    table = np.zeros((voxels, LANES), ml_dtypes.bfloat16)
    table[:, :GRAD_AT] = np.concatenate([squares] * PER_HALF).T
    plane_table = np.zeros((edge * edge, LANES), ml_dtypes.bfloat16)
    lines = np.concatenate([across] * (2 * ((comps + 1) // 2)))
    plane_table[:, GRAD_AT : GRAD_AT + len(lines)] = lines.T
    return table, plane_table, np.repeat(scale.astype(ml_dtypes.bfloat16), 16, axis=0)


def voxel_parts(voxels, sixteenths):
    ends = np.cumsum((0,) + sixteenths) * (voxels // 16)
    return tuple((int(a), int(b - a)) for a, b in zip(ends, ends[1:]))


def pair_place(i):
    return i // PER_HALF, i % PER_HALF * QUADS, QUADS


def gradient_place(c):
    return c % 2, GRAD_AT + c // 2 * NODES, NODES


@functools.cache
def packing(steps, comps):
    ends = [0, 0]
    places = [pair_place(i) for i in range(len(component_pairs(comps)))]
    for half, at, count in places + [gradient_place(c) for c in range(comps)]:
        ends[half] = max(ends[half], at + count)
    first = LANES - ends[0]
    rest = ends[1] - first
    assert 0 < 2 * rest < LANES
    pieces = []
    for k in range(steps):
        pieces += [
            (k, 0, 0, k, 0, ends[0]),
            (k, 1, 0, k, ends[0], first),
            (k, 1, first, shared_group(steps, k), k % 2 * rest, rest),
        ]
    return steps + (steps + 1) // 2, tuple(pieces)


def shared_group(steps, k):
    return steps + k // 2


def packed_lane(steps, pieces, step, half, lane):
    for s, h, source, group, goal, count in pieces:
        if (s, h) == (step, half) and source <= lane < source + count:
            return (group >= steps) * LANES + goal + lane - source


@functools.cache
def expansion_tables(steps, comps, edge):
    dofs = NODES * comps
    pairs = component_pairs(comps)
    _, pieces = packing(steps, comps)
    hessian = np.zeros((steps, 2 * LANES, dofs * dofs), ml_dtypes.bfloat16)
    gradient = np.zeros((steps, dofs, 2 * LANES), ml_dtypes.bfloat16)
    for k in range(steps):
        for d in range(dofs):
            a, c = divmod(d, comps)
            half, at, _ = gradient_place(c)
            for m in range(4):
                weight = 0.25
                for bit in range(2):
                    if m >> bit & 1:
                        weight *= (1 if a >> bit & 1 else -1) / edge
                lane = packed_lane(steps, pieces, k, half, at + (a >> 2) * 4 + m)
                gradient[k, d, lane] = weight
            for f in range(dofs):
                b, e = divmod(f, comps)
                quad = sum(((a >> n & 1) + (b >> n & 1)) * 3**n for n in range(3))
                half, at, _ = pair_place(pairs.index((min(c, e), max(c, e))))
                hessian[k, packed_lane(steps, pieces, k, half, at + quad), d * dofs + f] = 1
    return hessian, gradient


def spline_weights(phase):
    return [
        (1.0 - phase) ** 3 / 6.0,
        (3.0 * phase**3 - 6.0 * phase**2 + 4.0) / 6.0,
        (-3.0 * phase**3 + 3.0 * phase**2 + 3.0 * phase + 1.0) / 6.0,
        phase**3 / 6.0,
    ]


def column(row):
    n = row.shape[1]
    eye = lax.broadcasted_iota(jnp.int32, (n, n), 0) == lax.broadcasted_iota(jnp.int32, (n, n), 1)
    return jnp.sum(jnp.where(eye, jnp.broadcast_to(row, (n, n)), 0.0), axis=1, keepdims=True)


def moments_kernel(
    capacity,
    parts,
    grads_hbm,
    resid_hbm,
    counts_hbm,
    owner_hbm,
    phase_hbm,
    table_hbm,
    plane_table_hbm,
    scale_hbm,
    own_ref,
    send_a_ref,
    *refs,
):
    spaces = lax.axis_size("space")
    send_b_refs, refs = refs[:spaces], refs[spaces:]
    (
        grads,
        resid,
        counts_ref,
        owner_ref,
        phase_ref,
        table,
        plane_table,
        scale,
        products_a,
        products_b,
        limits,
        running,
        lines,
        sums,
        moments,
        small_sems,
        sems,
    ) = refs
    steps, comps, bricks, voxels = grads.shape
    pairs = component_pairs(comps)
    groups = len(pairs)
    rows = steps * bricks
    plane = round(voxels ** (2 / 3))
    buffers = (products_a, products_b)
    small = [
        pltpu.make_async_copy(src, dst, small_sems.at[i])
        for i, (src, dst) in enumerate(
            [
                (counts_hbm, counts_ref),
                (owner_hbm, owner_ref),
                (phase_hbm, phase_ref),
                (scale_hbm, scale),
                (plane_table_hbm, plane_table),
            ]
        )
    ]

    def copies(k):
        start, width = parts[k]
        cols = pl.ds(start, width)
        return (
            pltpu.make_async_copy(grads_hbm.at[:, :, :, cols], grads.at[:, :, :, cols], sems.at[k, 0]),
            pltpu.make_async_copy(resid_hbm.at[:, :, cols], resid.at[:, :, cols], sems.at[k, 1]),
            pltpu.make_async_copy(table_hbm.at[cols], table.at[cols], sems.at[k, 2]),
        )

    for copy in small:
        copy.start()
    for k in range(len(parts)):
        for copy in copies(k):
            copy.start(priority=min(k, 1))

    lane = lax.broadcasted_iota(jnp.int32, (1, LANES), 1)
    tall = math.gcd(bricks, 16)
    voxel = lax.broadcasted_iota(jnp.int16, (tall, plane), 1)
    zero = jnp.zeros((), BF16)

    edge = voxels // plane

    def fill(k, products):
        start, width = parts[k]
        for b in range(0, bricks, tall):
            limit = (limits[b : b + tall] - start).astype(jnp.int16)
            for s in range(steps):
                total = [running[0, c, s, b : b + tall] for c in range(comps)] if k else None
                ramp = [running[1, c, s, b : b + tall] for c in range(comps)] if k else None
                for p in range(0, width, plane):
                    cols = slice(start + p, start + p + plane)
                    valid = voxel + jnp.int16(p) < limit
                    scale_here = jnp.where(valid, scale[:tall, cols], zero)
                    resid_here = jnp.where(valid, resid[s, b : b + tall, cols], zero).astype(F32)
                    g = [grads[s, c, b : b + tall, cols] for c in range(comps)]
                    scaled = [x * scale_here for x in g]
                    for i, (c, e) in enumerate(pairs):
                        at = i * rows + s * bricks + b
                        products[at : at + tall, p : p + plane] = scaled[c] * g[e]
                    terms = [x.astype(F32) * resid_here for x in g]
                    total = terms if total is None else [x + y for x, y in zip(total, terms)]
                    ramp = total if ramp is None else [x + y for x, y in zip(ramp, total)]
                for c in range(comps):
                    if k + 1 < len(parts):
                        running[0, c, s, b : b + tall] = total[c]
                        running[1, c, s, b : b + tall] = ramp[c]
                        continue
                    falling = (ramp[c] - 0.5 * total[c]) * (1.0 / edge)
                    for n, line in enumerate((falling, total[c] - falling)):
                        at = ((n * comps + c) * steps + s) * bricks + b
                        for m, part in enumerate(split(line)):
                            lines[m, at : at + tall] = part

    def reduce(k, products):
        start, width = parts[k]
        for at in range(0, groups * rows, groups * rows // 2):
            here = slice(at, at + groups * rows // 2)
            part = jnp.dot(products[here, :width], table[start : start + width], preferred_element_type=F32)
            sums[here] = part if k == 0 else sums[here] + part

    for copy in small:
        copy.wait()
    counts = column(counts_ref[...].astype(F32)).astype(jnp.int32)
    limits[...] = jnp.broadcast_to(counts, (bricks, plane))
    owner_row = owner_ref[...].astype(F32)
    owner_col = column(owner_row)
    square = (bricks, bricks)
    earlier = lax.broadcasted_iota(jnp.int32, square, 1) < lax.broadcasted_iota(jnp.int32, square, 0)
    same = (owner_col == owner_row) & earlier
    rank = jnp.sum(jnp.where(same, 1.0, 0.0), axis=1, keepdims=True)
    destination = owner_col * capacity + rank
    later = lax.broadcasted_iota(jnp.int32, square, 1) > lax.broadcasted_iota(jnp.int32, square, 0)
    before = jnp.where((owner_col == owner_row) & later, 1.0, 0.0)
    destination_row = owner_row * capacity + jnp.sum(before, axis=0, keepdims=True)
    me = lax.axis_index("space")
    slot = lax.broadcasted_iota(jnp.int32, (capacity, bricks), 0)
    picks = []
    for distance in range(spaces):
        goal = (slot + (me + distance) % spaces * capacity).astype(F32)
        picks.append(jnp.where(goal == destination_row, 1.0, 0.0).astype(BF16))

    place = lax.axis_index("tm")
    places = lax.axis_size("tm")
    first_step = place * steps
    odd = place % 2 == 1
    weights = [spline_weights(phase_ref[:, s : s + 1]) for s in range(steps)]
    factors = {}
    for s in range(steps):
        for position in range(-1, steps + 2):
            basis = None
            for j in range(4):
                reach = s - 1 + j
                if position not in (reach, max(reach, 0), min(reach, steps - 1)):
                    continue
                goal = jnp.clip(first_step + reach, 0, places * steps - 1) - first_step
                term = jnp.where(goal == position, weights[s][j], 0.0)
                basis = term if basis is None else basis + term
            if basis is not None:
                factors[position, s] = jnp.where(lane < GRAD_AT, basis * basis, basis)

    def coefficient(position):
        return [
            sum(
                factors[position, s] * moments[s, :, half * LANES : (half + 1) * LANES]
                for s in range(steps)
                if (position, s) in factors
            )
            for half in range(2)
        ]

    for k in range(len(parts)):
        for copy in copies(k):
            copy.wait()
        fill(k, buffers[k % 2])
        reduce(k, buffers[k % 2])

    line_sums = sum(
        jnp.dot(lines[m], plane_table[...], preferred_element_type=F32) for m in range(2)
    )
    for s in range(steps):
        halves = [jnp.zeros((bricks, LANES), F32) for _ in range(2)]
        for i in range(len(pairs)):
            half, goal, span = pair_place(i)
            at = i * rows + s * bricks
            keep = (lane >= goal) & (lane < goal + span)
            halves[half] = jnp.where(keep, sums[at : at + bricks], halves[half])
        for c in range(comps):
            half, goal, span = gradient_place(c)
            for n in range(2):
                at = (n * comps + c) * rows + s * bricks
                first = goal + n * span // 2
                keep = (lane >= first) & (lane < first + span // 2)
                halves[half] = jnp.where(keep, line_sums[at : at + bricks], halves[half])
        for half in range(2):
            moments[s, :, half * LANES : (half + 1) * LANES] = halves[half]

    packed_groups, pieces = packing(steps, comps)

    def pack(slabs):
        packed = [jnp.zeros((bricks, LANES), F32) for _ in range(packed_groups)]
        for k, half, source, group, goal, count in pieces:
            if slabs[k] is None:
                continue
            block = slabs[k][half]
            if goal != source:
                block = pltpu.roll(block, (goal - source) % LANES, 1)
            keep = (lane >= goal) & (lane < goal + count)
            packed[group] = jnp.where(keep, block, packed[group])
        return packed

    above = pack([coefficient(steps + k) if k < 2 else None for k in range(steps)])
    below = pack([coefficient(-1) if k == steps - 1 else None for k in range(steps)])
    pick = jnp.concatenate(picks, axis=0)
    for group in range(packed_groups):
        cols = slice(group * LANES, (group + 1) * LANES)
        parts_b = split(jnp.where(odd, above[group], below[group]))
        both = jnp.dot(pick, jnp.concatenate(parts_b, axis=1), preferred_element_type=F32)
        placed = both[:, :LANES] + both[:, LANES:]
        for distance, ref in enumerate(send_b_refs):
            ref[:, cols] = placed[distance * capacity : (distance + 1) * capacity]
        send_a_ref[:, cols] = jnp.where(odd, below[group], above[group])
    mine = pack([coefficient(k) for k in range(steps)])
    mine[-1] = jnp.where(lane == LANES - 1, destination, mine[-1])
    for group in range(packed_groups):
        own_ref[:, group * LANES : (group + 1) * LANES] = mine[group]


def split(x):
    high = x.astype(BF16)
    return high, (x - high.astype(F32)).astype(BF16)


def place_kernel(capacity, *refs):
    *blocks, out_ref = refs
    me = lax.axis_index("space")
    width = out_ref.shape[1]
    for distance, block in enumerate(blocks):
        slot = lax.broadcasted_iota(jnp.int32, (block.shape[0], capacity), 1)
        goal = (slot + me * capacity).astype(F32)
        pick = jnp.where(goal == block[:, width - 1 :], 1.0, 0.0).astype(BF16)
        out_ref[distance * capacity : (distance + 1) * capacity] = sum(
            lax.dot_general(pick, part, (((0,), (0,)), ((), ())), preferred_element_type=F32)
            for part in split(block[...])
        )


def expand_kernel(
    capacity, ready, last, table, gradient_table, hessian_hbm, gradient_hbm, total, wide, thin, sems
):
    steps, slots, _ = wide.shape
    spaces = slots // capacity
    me = lax.axis_index("space")
    for distance in range(spaces):
        here = slice(distance * capacity, (distance + 1) * capacity)
        source = (me + spaces - distance) % spaces
        rows = pl.ds(pl.multiple_of(source * capacity, math.gcd(capacity, 8)), capacity)
        total[rows] = ready[here] + last[here]
    copies = []
    parts = []
    for k in range(steps):
        lanes = [slice(g * LANES, (g + 1) * LANES) for g in (k, shared_group(steps, k))]
        parts.append(split(jnp.concatenate([total[:, cols] for cols in lanes], axis=1)))
        wide[k] = sum(jnp.dot(part, table[k], preferred_element_type=F32) for part in parts[k])
        copies.append(pltpu.make_async_copy(wide.at[k], hessian_hbm.at[k], sems.at[k]))
        copies[-1].start()
    for k in range(steps):
        thin[k] = sum(
            lax.dot_general(gradient_table[k], part, (((1,), (1,)), ((), ())), preferred_element_type=F32)
            for part in parts[k]
        )
    copies.append(pltpu.make_async_copy(thin, gradient_hbm, sems.at[steps]))
    copies[-1].start()
    for copy in copies:
        copy.wait()


def per_device(image_gradient, residual, phase, counts, owner):
    steps, bricks, comps, voxels = image_gradient.shape
    spaces = lax.axis_size("space")
    places = lax.axis_size("tm")
    capacity = 3 * bricks // (2 * spaces)
    dofs = NODES * comps
    groups = len(component_pairs(comps))
    plane = round(voxels ** (2 / 3))
    parts = voxel_parts(voxels, (3, 6, 5, 2))
    widest = max(width for _, width in parts)
    table, plane_table, scale = voxel_tables(voxels, comps)
    block = (bricks, packing(steps, comps)[0] * LANES)
    in_hbm = pl.BlockSpec(memory_space=pltpu.HBM)
    own, send_a, *send_b = pl.pallas_call(
        functools.partial(moments_kernel, capacity, parts),
        in_specs=[in_hbm] * 8,
        out_shape=[pltpu.VMEM(block, F32)] * 2 + [pltpu.VMEM((capacity, block[1]), F32)] * spaces,
        scratch_shapes=[
            pltpu.VMEM((steps, comps, bricks, voxels), BF16),
            pltpu.VMEM((steps, bricks, voxels), BF16),
            pltpu.VMEM((1, bricks), jnp.int32),
            pltpu.VMEM((1, bricks), jnp.int32),
            pltpu.VMEM((1, steps), F32),
            pltpu.VMEM((voxels, LANES), BF16),
            pltpu.VMEM((plane, LANES), BF16),
            pltpu.VMEM(scale.shape, BF16),
            pltpu.VMEM((groups * steps * bricks, widest), BF16),
            pltpu.VMEM((groups * steps * bricks, widest), BF16),
            pltpu.VMEM((bricks, plane), jnp.int32),
            pltpu.VMEM((2, comps, steps, bricks, plane), F32),
            pltpu.VMEM((2, 2 * comps * steps * bricks, plane), BF16),
            pltpu.VMEM((groups * steps * bricks, LANES), F32),
            pltpu.VMEM((steps, bricks, 2 * LANES), F32),
            pltpu.SemaphoreType.DMA((5,)),
            pltpu.SemaphoreType.DMA((len(parts), 3)),
        ],
        compiler_params=pltpu.CompilerParams(vmem_limit_bytes=32 << 20),
        name="moments",
    )(
        *(
            pltpu.with_memory_space_constraint(x, pltpu.HBM)
            for x in (
                jnp.transpose(image_gradient, (0, 2, 1, 3)),
                residual,
                counts.reshape(1, bricks),
                owner.reshape(1, bricks),
                phase.reshape(1, steps),
                jnp.asarray(table),
                jnp.asarray(plane_table),
                jnp.asarray(scale),
            )
        )
    )

    def exchange(values, start):
        lower = range(start, places - 1, 2)
        route = [(i, i + 1) for i in lower] + [(i + 1, i) for i in lower]
        return lax.ppermute(values, "tm", route) if route else jnp.zeros_like(values)

    def turned(values, distance):
        route = [(i, (i + distance) % spaces) for i in range(spaces)]
        return lax.ppermute(values, "space", route) if distance else values

    for_far = jnp.concatenate([turned(x, distance) for distance, x in enumerate(send_b)])
    near = own + exchange(send_a, 0)
    last = exchange(for_far, 1)
    blocks = [turned(near, distance) for distance in range(spaces)]
    slots = spaces * capacity
    ready = pl.pallas_call(
        functools.partial(place_kernel, capacity),
        out_shape=pltpu.VMEM((slots, block[1]), F32),
        compiler_params=pltpu.CompilerParams(vmem_limit_bytes=8 << 20),
        name="place",
    )(*blocks)
    hessian_table, gradient_table = (jnp.asarray(x) for x in expansion_tables(steps, comps, round(voxels ** (1 / 3))))
    wide = (steps, slots, dofs * dofs)
    thin = (steps, dofs, slots)
    hessian, gradient = pl.pallas_call(
        functools.partial(expand_kernel, capacity),
        out_shape=[jax.ShapeDtypeStruct(wide, F32), jax.ShapeDtypeStruct(thin, F32)],
        out_specs=[in_hbm] * 2,
        scratch_shapes=[
            pltpu.VMEM((slots, block[1]), F32),
            pltpu.VMEM(wide, F32),
            pltpu.VMEM(thin, F32),
            pltpu.SemaphoreType.DMA((steps + 1,)),
        ],
        compiler_params=pltpu.CompilerParams(vmem_limit_bytes=16 << 20),
        name="expand",
    )(ready, last, hessian_table, gradient_table)
    return hessian, jnp.transpose(gradient, (0, 2, 1))


def solution(mesh):
    in_specs = (
        P("tm", "space", None, None),
        P("tm", "space", None),
        P("tm"),
        P("space"),
        P("space", None),
    )
    out_specs = (P("tm", "space", None), P("tm", "space", None))
    return jax.shard_map(
        per_device, mesh=mesh, in_specs=in_specs, out_specs=out_specs, check_vma=False
    )
```
